512 devices in a mesh: var: 32 (over y_lo, z), lon: 16 (over x, y_hi, core).
Axes of the slice: x: 4, y: 8 (y_hi: 2, y_lo: 4; y = y_hi * 4 + y_lo), z: 8, core: 2. Of those that a mesh axis runs over, the one named last changes fastest.
Arguments:
- pixels: bfloat16 [32, 768, 768], P('var', None, 'lon'), may hold values from -50 to 50
- embed_weight: bfloat16 [4, 16, 512], replicated, may hold values from -0.75 to 0.75
- level_code: float32 [8, 512], replicated, may hold values from -6 to 6
- queries: bfloat16 [3, 512], replicated, may hold values from -6 to 6
- w_key: bfloat16 [512, 512], replicated, may hold values from -0.25 to 0.25
- w_value: bfloat16 [512, 512], replicated, may hold values from -0.25 to 0.25
- w_out: bfloat16 [512, 512], replicated, may hold values from -0.25 to 0.25
- w_qkv: bfloat16 [512, 1536], replicated, may hold values from -0.25 to 0.25
- w_proj: bfloat16 [512, 512], replicated, may hold values from -0.25 to 0.25
Outputs:
- encoded: bfloat16 [3, 192, 192, 512], P(None, 'var', 'lon')
The draws below stay inside these ranges and needn't reach their ends.
All inputs are finite; a program needn't handle non-finite values.
Results may differ from the reference program's by a relative error of at most 0.017.
Values may be sent and summed in bfloat16 or wider, within the bound.
No kernel may reach another device: no remote copies, remote signals or barrier semaphores. Data moves between devices by JAX's collectives and lax.ppermute only.
A program may use at most 64 MiB of HBM per device.

```python
import math
import jax
import jax.numpy as jnp
from jax import lax

D = 512
HEAD = 64
ATM_VARS = 4
LATENT = 3
WLAT = 6
WLON = 12
FIELDS = 32
LEVELS = 8
NLAT = 192
NLON = 192


def draw_pixels(key, part):
    key = jax.random.fold_in(key, 11)
    key_base, key_field, key_row = jax.random.split(key, 3)
    shape = (FIELDS, NLAT * 4, NLON * 4)
    base = jnp.clip(jax.random.normal(key_base, shape, jnp.float32), -4.0, 4.0)
    field_scale = jnp.exp(jax.random.uniform(key_field, (FIELDS, 1, 1), jnp.float32, 0.0, math.log(3.2)))
    row_scale = jnp.exp(jax.random.uniform(key_row, (1, NLAT * 4, 1), jnp.float32, 0.0, math.log(3.2)))
    return (base * field_scale * row_scale).astype(jnp.bfloat16)


def centred(key, extent, deviation, bound, dtype=jnp.bfloat16):
    return jnp.clip(deviation * jax.random.normal(key, extent, jnp.float32), -bound, bound).astype(dtype)


def setup_inputs(seed: int = 0) -> dict:
    key_list = jax.random.split(jax.random.key(seed), 10)
    pixels = draw_pixels(jax.random.fold_in(key_list[9], 71), 0)
    embed_weight = centred(key_list[1], (ATM_VARS, 16, D), (16 * ATM_VARS) ** -0.5, 0.75)
    level_code = centred(key_list[2], (LEVELS, D), 1.0, 6.0, jnp.float32)
    queries = centred(key_list[3], (LATENT, D), 1.0, 6.0)
    w_key = centred(key_list[4], (D, D), D ** -0.5, 0.25)
    w_value = centred(key_list[5], (D, D), D ** -0.5, 0.25)
    w_out = centred(key_list[6], (D, D), D ** -0.5, 0.25)
    w_qkv = centred(key_list[7], (D, 3 * D), D ** -0.5, 0.25)
    w_proj = centred(key_list[8], (D, D), D ** -0.5, 0.25)
    return {"pixels": pixels, "embed_weight": embed_weight, "level_code": level_code, "queries": queries, "w_key": w_key, "w_value": w_value, "w_out": w_out, "w_qkv": w_qkv, "w_proj": w_proj}


def norm_rows(values_in):
    center = values_in - lax.optimization_barrier(jnp.mean(values_in, axis=-1, keepdims=True))
    spread = lax.optimization_barrier(jnp.mean(center * center, axis=-1, keepdims=True))
    return center * lax.rsqrt(spread + 1e-05)

def to_patches(pixel_block):
    count, rows, cols = pixel_block.shape
    shaped = pixel_block.reshape(count, rows // 4, 4, cols // 4, 4)
    return shaped.transpose(0, 1, 3, 2, 4).reshape(count, rows // 4, cols // 4, 16)

def embed(patch_block, field_weights):
    product = jnp.einsum('fabk,fkd->fabd', patch_block.astype(jnp.float32), field_weights.astype(jnp.float32))
    return product.astype(jnp.bfloat16)

def aggregate(embedded, level_code, queries, w_key, w_value, w_out):
    count, rows, cols, width = embedded.shape
    levels = level_code.shape[0]
    heads = width // HEAD
    token = embedded.astype(jnp.float32).reshape(levels, count // levels, rows, cols, width).sum(axis=1)
    token = token + level_code[:, None, None, :]
    normed = norm_rows(token).astype(jnp.bfloat16).reshape(-1, width)
    keys = jnp.dot(normed, w_key, preferred_element_type=jnp.float32).astype(jnp.bfloat16)
    values = jnp.dot(normed, w_value, preferred_element_type=jnp.float32).astype(jnp.bfloat16)
    keys = keys.reshape(levels, rows, cols, heads, HEAD).astype(jnp.float32)
    values = values.reshape(levels, rows, cols, heads, HEAD).astype(jnp.float32)
    query_heads = queries.reshape(LATENT, heads, HEAD).astype(jnp.float32)
    scores = jnp.einsum('qhe,labhe->abhql', query_heads, keys) * HEAD ** (-0.5)
    expo = jnp.exp(scores)
    level_weights = (expo / lax.optimization_barrier(jnp.sum(expo, axis=-1, keepdims=True))).astype(jnp.bfloat16)
    attended = jnp.einsum('abhql,labhe->qabhe', level_weights.astype(jnp.float32), values)
    attended = attended.astype(jnp.bfloat16).reshape(-1, width)
    projected = jnp.dot(attended, w_out, preferred_element_type=jnp.float32).reshape(LATENT, rows, cols, width)
    return (queries.astype(jnp.float32)[:, None, None, :] + projected).astype(jnp.bfloat16)

def window_layer(latent, w_qkv, w_proj):
    levels, rows, cols, width = latent.shape
    heads = width // HEAD
    row_blocks = rows // WLAT
    col_blocks = cols // WLON
    windows = latent.reshape(levels, row_blocks, WLAT, col_blocks, WLON, width).transpose(1, 3, 0, 2, 4, 5)
    windows = windows.reshape(row_blocks * col_blocks, levels * WLAT * WLON, width)
    count, members, _ = windows.shape
    normed = norm_rows(windows.astype(jnp.float32)).astype(jnp.bfloat16).reshape(-1, width)
    qkv = jnp.dot(normed, w_qkv, preferred_element_type=jnp.float32).astype(jnp.bfloat16)
    qkv = qkv.reshape(count, members, 3, heads, HEAD).astype(jnp.float32)
    scores = jnp.einsum('wnhe,wmhe->whnm', qkv[:, :, 0], qkv[:, :, 1]) * HEAD ** (-0.5)
    expo = jnp.exp(scores)
    probs = (expo / lax.optimization_barrier(jnp.sum(expo, axis=-1, keepdims=True))).astype(jnp.bfloat16)
    mixed = jnp.einsum('whnm,wmhe->wnhe', probs.astype(jnp.float32), qkv[:, :, 2]).astype(jnp.bfloat16)
    projected = jnp.dot(mixed.reshape(-1, width), w_proj, preferred_element_type=jnp.float32)
    summed = (windows.astype(jnp.float32).reshape(-1, width) + projected).astype(jnp.bfloat16)
    summed = summed.reshape(row_blocks, col_blocks, levels, WLAT, WLON, width).transpose(2, 0, 3, 1, 4, 5)
    return summed.reshape(levels, rows, cols, width)

def reference(pixels, embed_weight, level_code, queries, w_key, w_value, w_out, w_qkv, w_proj):
    fields = pixels.shape[0]
    bands = NLAT // WLAT
    field_weights = jnp.tile(embed_weight, (LEVELS, 1, 1))
    stacked = pixels.reshape(fields, bands, WLAT * 4, NLON * 4).transpose(1, 0, 2, 3)

    def one_band(band):
        latent = aggregate(embed(to_patches(band), field_weights), level_code, queries, w_key, w_value, w_out)
        latent = jnp.roll(latent, -(WLON // 2), axis=2)
        return window_layer(latent, w_qkv, w_proj)
    result = lax.map(one_band, stacked)
    return result.transpose(1, 0, 2, 3, 4).reshape(LATENT, NLAT, NLON, D)
```

```python
import jax
import jax.numpy as jnp
from jax import lax
from jax.experimental import pallas as pl
from jax.experimental.pallas import tpu as pltpu
from jax.sharding import PartitionSpec as P

HEAD = 64
LATENT = 3
WLAT = 6
WLON = 12
HALF = WLON // 2
PATCH = 4
SLOT = 8
LANES = 128
GROUP = 32
LOG2E = 1.4426950408889634
F32 = jnp.float32
BF16 = jnp.bfloat16


def mul(a, b):
    return jnp.dot(a, b, preferred_element_type=F32)


def mul_t(a, b):
    return lax.dot_general(a, b, (((1,), (1,)), ((), ())), preferred_element_type=F32)


def iota(shape, dim):
    return lax.broadcasted_iota(jnp.int32, shape, dim)


def split(value):
    high = value.astype(BF16).astype(F32)
    return high, value - high


def pack_kernel(pixel_ref, out_ref, rows):
    count, cols = pixel_ref.shape
    band = PATCH * WLAT
    bands = count // band
    rows[pl.ds(0, count), pl.ds(0, cols)] = pixel_ref[...].astype(F32)
    rows[pl.ds(count, 16), :] = jnp.zeros((16, LANES), F32)
    source, target = iota((cols, 2 * LANES), 0), iota((cols, 2 * LANES), 1)
    base = source // (cols // 2) * LANES + source % (cols // 2)
    total = None
    for r in range(PATCH):
        picked = jnp.concatenate(
            [rows[pl.ds(band * g + r, SLOT, stride=PATCH), :] for g in range(bands)], axis=0
        )[:, :cols].astype(BF16)
        place = jnp.where(target == base + r * GROUP, 1.0, 0.0).astype(BF16)
        part = mul(picked, place)
        total = part if total is None else total + part
    west = total[:, :LANES].reshape(bands, SLOT, LANES)
    own = total[:, LANES:].reshape(bands, SLOT, LANES)
    out_ref[...] = (
        jnp.concatenate([west, own], axis=1).reshape(bands * 2 * SLOT, LANES).astype(BF16)
    )


def fold_weights(embed_ref, level_ref, query_ref, key_ref, value_ref):
    pixels, width = embed_ref.shape
    levels = level_ref.shape[0]
    ext = jnp.concatenate([embed_ref[...].astype(F32), level_ref[...]], axis=0)
    count = pixels + levels
    ext = ext - jnp.mean(ext, axis=-1, keepdims=True)
    high, low = split(ext)
    stacked = jnp.concatenate([high, low], axis=0).astype(BF16)
    keys = mul(stacked, key_ref[...])
    keys = keys[:count] + keys[count:]
    values = mul(stacked, value_ref[...])
    values = values[:count] + values[count:]
    heads = width // HEAD
    scores = None
    for q in range(LATENT):
        high_q, low_q = split(keys * query_ref[pl.ds(q, 1), :].astype(F32))
        both = jnp.concatenate([high_q, low_q], axis=0).astype(BF16)
        collect = jnp.where(
            iota((width, LANES), 1) == q * heads + iota((width, LANES), 0) // HEAD, 1.0, 0.0
        ).astype(BF16)
        part = mul(both, collect)
        part = part[:count] + part[count:]
        scores = part if scores is None else scores + part
    scores = scores * (HEAD ** (-0.5) * LOG2E)
    zeros = jnp.zeros((LANES - count, width), F32)
    high_t = jnp.concatenate([high, zeros], axis=0).astype(BF16)
    low_t = jnp.concatenate([low, zeros], axis=0).astype(BF16)
    high_b, low_b = high.astype(BF16), low.astype(BF16)
    gram = (mul_t(high_b, high_t) + (mul_t(high_b, low_t) + mul_t(low_b, high_t))) * (1.0 / width)
    row, lane = iota((count, LANES), 0), iota((count, LANES), 1)
    diagonal = jnp.sum(jnp.where(row == lane, gram, 0.0), axis=-1, keepdims=True)
    spread = jnp.where(row < pixels, gram, 2.0 * gram)
    spread = jnp.where(
        lane < pixels, spread, jnp.where((lane == pixels) & (row >= pixels), diagonal, 0.0)
    )
    folded = jnp.concatenate([values, spread, scores], axis=1)
    high_f, low_f = split(folded)
    rest = jnp.zeros((2 * LANES - 2 * count, folded.shape[1]), F32)
    return jnp.concatenate(
        [high_f[:pixels], low_f[:pixels], high_f[pixels:], low_f[pixels:], rest], axis=0
    ).astype(BF16)


def aggregate_half(rows, folded, query_ref, out_weight, levels):
    variables = rows.shape[0] // levels
    width = out_weight.shape[0]
    heads = width // HEAD
    pixels = variables * PATCH * PATCH
    grid = rows.reshape(levels, variables, SLOT, LANES)
    wide = jnp.concatenate(
        [grid[:, v].reshape(levels * SLOT, LANES) for v in range(variables)], axis=1
    )
    depth = variables * LANES
    column = iota((1, depth), 1) % GROUP // PATCH
    masked = jnp.concatenate(
        [jnp.where(column == b, wide, 0.0) for b in range(HALF)], axis=0
    ).astype(BF16)
    source, target = iota((depth, LANES), 0), iota((depth, LANES), 1)
    place = (
        source // LANES * (PATCH * PATCH) + source % LANES // GROUP * PATCH + source % PATCH
    )
    gather = jnp.where(target % pixels == place, 1.0, 0.0).astype(BF16)
    patch = mul(masked, gather)
    count = HALF * levels * SLOT
    row, lane = iota((count, LANES), 0), iota((count, LANES), 1)
    level = jnp.where(
        (lane < 2 * levels) & (lane % levels == row // SLOT % levels), 1.0, 0.0
    )
    full = jnp.concatenate([patch, level], axis=1).astype(BF16)
    product = mul(full, folded)
    values = product[:, :width]
    spread = product[:, width : width + LANES]
    scores = product[:, width + LANES :]
    variance = jnp.sum(jnp.where(lane == pixels, 1.0, patch) * spread, axis=-1, keepdims=True)
    scale = lax.rsqrt(jnp.maximum(variance, 0.0) + 1e-05)
    expo = jnp.exp2(scores * scale).reshape(HALF, levels, SLOT, LANES)
    weights = expo / jnp.sum(expo, axis=1, keepdims=True) * scale.reshape(HALF, levels, SLOT, 1)
    weights = weights.reshape(count, LANES).astype(BF16)
    mixed = []
    for q in range(LATENT):
        spread_out = jnp.where(
            iota((LANES, width), 0) == q * heads + iota((LANES, width), 1) // HEAD, 1.0, 0.0
        ).astype(BF16)
        part = mul(weights, spread_out) * values
        mixed.append(part.reshape(HALF, levels, SLOT, width).sum(axis=1).reshape(HALF * SLOT, width))
    attended = jnp.concatenate(mixed, axis=0).astype(BF16)
    latent = mul(attended, out_weight).reshape(LATENT, HALF * SLOT, width)
    latent = latent + query_ref[...].astype(F32)[:, None, :]
    return latent.astype(BF16).astype(F32)


def own_kernel(
    block_ref, embed_ref, level_ref, query_ref, key_ref, value_ref, out_w_ref, latent_ref, folded_ref
):
    folded = fold_weights(embed_ref, level_ref, query_ref, key_ref, value_ref)
    folded_ref[...] = folded
    fields = block_ref.shape[0] // (2 * SLOT)
    rows = block_ref[...].astype(F32).reshape(fields, 2, SLOT, LANES)[:, 1]
    latent_ref[...] = aggregate_half(rows, folded, query_ref, out_w_ref[...], level_ref.shape[0])


def window_kernel(
    block_ref, own_ref, folded_ref, query_ref, out_w_ref, qkv_w_ref, proj_w_ref, out_ref, slots, clean
):
    fields = block_ref.shape[0] // SLOT
    width = out_w_ref.shape[0]
    levels = fields // 4
    rows = block_ref[...].astype(F32).reshape(fields, SLOT, LANES)
    east = aggregate_half(rows, folded_ref[...], query_ref, out_w_ref[...], levels)
    half_rows = HALF * SLOT
    for q in range(LATENT):
        for c in range(width // LANES):
            part = pl.ds(c * LANES, LANES)
            slots[c, pl.ds(q * 2 * half_rows, half_rows), :] = own_ref[q, :, part]
            slots[c, pl.ds(q * 2 * half_rows + half_rows, half_rows), :] = east[
                q, :, c * LANES : (c + 1) * LANES
            ]
    for q in range(LATENT):
        for a in range(WLAT):
            for c in range(width // LANES):
                clean[pl.ds((q * WLAT + a) * WLON, WLON), pl.ds(c * LANES, LANES)] = slots[
                    c, pl.ds(q * 2 * half_rows + a, WLON, stride=SLOT), :
                ]
    members = LATENT * WLAT * WLON
    shifted = clean[...]
    center = shifted - jnp.mean(shifted, axis=-1, keepdims=True)
    spread = jnp.mean(center * center, axis=-1, keepdims=True)
    normed = (center * lax.rsqrt(spread + 1e-05)).astype(BF16)
    qkv = mul(normed, qkv_w_ref[...]).astype(BF16)
    first = iota((1, LANES), 1) < HEAD
    mixed = []
    for p in range(width // LANES):
        queries = qkv[:, p * LANES : (p + 1) * LANES]
        keys = qkv[:, width + p * LANES : width + (p + 1) * LANES]
        values = qkv[:, 2 * width + p * LANES : 2 * width + (p + 1) * LANES]
        values = jnp.concatenate(
            [values * BF16(2.0**-8), jnp.ones((members, LANES), BF16)], axis=1
        )
        found = []
        for keep in (first, jnp.logical_not(first)):
            chosen = jnp.where(keep, queries, jnp.zeros_like(queries))
            scores = mul_t(chosen, keys)
            expo = jnp.exp2(scores * (HEAD ** (-0.5) * LOG2E)).astype(BF16)
            found.append(mul(expo, values))
        both = jnp.where(jnp.concatenate([first, first], axis=1), found[0], found[1])
        mixed.append((both[:, :LANES] / both[:, LANES:] * 2.0**8).astype(BF16))
    projected = mul(jnp.concatenate(mixed, axis=1), proj_w_ref[...])
    clean[...] = shifted + projected
    for q in range(LATENT):
        for a in range(WLAT):
            out_ref[q, a] = clean[pl.ds((q * WLAT + a) * WLON, WLON), :].astype(BF16)


def whole(count):
    return [pl.BlockSpec(memory_space=pltpu.VMEM)] * count


def body(pixels, embed_weight, level_code, queries, w_key, w_value, w_out, w_qkv, w_proj):
    _, count, cols = pixels.shape
    bands = count // (PATCH * WLAT)
    width = w_out.shape[0]
    packed = pl.pallas_call(
        pack_kernel,
        out_shape=jax.ShapeDtypeStruct((bands * 2 * SLOT, LANES), BF16),
        in_specs=whole(1),
        out_specs=whole(1)[0],
        scratch_shapes=[pltpu.VMEM((count + 16, LANES), F32)],
        name="pack",
    )(pixels[0])
    block = lax.all_to_all(
        packed.reshape(bands, 2 * SLOT, LANES), "var", split_axis=0, concat_axis=0, tiled=True
    )
    sectors = lax.axis_size("lon")
    east = lax.ppermute(block[:, :SLOT], "lon", [(i, (i - 1) % sectors) for i in range(sectors)])
    fields = block.shape[0]
    own, folded = pl.pallas_call(
        own_kernel,
        out_shape=[
            jax.ShapeDtypeStruct((LATENT, HALF * SLOT, width), F32),
            jax.ShapeDtypeStruct((2 * LANES, width + 2 * LANES), BF16),
        ],
        in_specs=whole(7),
        out_specs=whole(2),
        compiler_params=pltpu.CompilerParams(vmem_limit_bytes=24 * 2**20),
        cost_estimate=pl.CostEstimate(flops=4 * 10**9, bytes_accessed=2 * 10**6, transcendentals=0),
        name="own_half",
    )(
        block.reshape(fields * 2 * SLOT, LANES),
        embed_weight.reshape(-1, width),
        level_code,
        queries,
        w_key,
        w_value,
        w_out,
    )
    return pl.pallas_call(
        window_kernel,
        out_shape=jax.ShapeDtypeStruct((LATENT, WLAT, WLON, width), BF16),
        in_specs=whole(7),
        out_specs=whole(1)[0],
        scratch_shapes=[
            pltpu.VMEM((width // LANES, LATENT * WLON * SLOT, LANES), F32),
            pltpu.VMEM((LATENT * WLAT * WLON, width), F32),
        ],
        compiler_params=pltpu.CompilerParams(vmem_limit_bytes=32 * 2**20),
        cost_estimate=pl.CostEstimate(flops=8 * 10**9, bytes_accessed=4 * 10**6, transcendentals=0),
        name="window",
    )(east.reshape(fields * SLOT, LANES), own, folded, queries, w_out, w_qkv, w_proj)


def solution(mesh):
    placed = (P("var", None, "lon"), P(), P(), P(), P(), P(), P(), P(), P())
    return jax.shard_map(
        body, mesh=mesh, in_specs=placed, out_specs=P(None, "var", "lon", None), check_vma=False
    )
```

```python
import jax
import jax.numpy as jnp
from jax import lax
from jax.experimental import pallas as pl
from jax.experimental.pallas import tpu as pltpu
from jax.sharding import PartitionSpec as P

HEAD = 64
LATENT = 3
WLAT = 6
WLON = 12
HALF = WLON // 2
PATCH = 4
SLOT = 8
LANES = 128
GROUP = 32
LOG2E = 1.4426950408889634
F32 = jnp.float32
BF16 = jnp.bfloat16


def mul(a, b):
    return jnp.dot(a, b, preferred_element_type=F32)


def mul_t(a, b):
    return lax.dot_general(a, b, (((1,), (1,)), ((), ())), preferred_element_type=F32)


def iota(shape, dim):
    return lax.broadcasted_iota(jnp.int32, shape, dim)


def split(value):
    high = value.astype(BF16).astype(F32)
    return high, value - high


def pack_kernel(pixel_ref, out_ref, placed):
    cols, count = pixel_ref.shape
    band = PATCH * WLAT
    bands = count // band
    source, target = iota((cols, 2 * LANES), 0), iota((cols, 2 * LANES), 1)
    place = (target // LANES == source // (cols // 2)) & (target % GROUP == source % (cols // 2))
    wide = lax.dot_general(
        pixel_ref[...],
        jnp.where(place, 1.0, 0.0).astype(BF16),
        (((0,), (0,)), ((), ())),
        preferred_element_type=F32,
    )
    for h in range(2):
        placed[h, pl.ds(0, count), :] = wide[:, h * LANES : (h + 1) * LANES]
        placed[h, pl.ds(count, 16), :] = jnp.zeros((16, LANES), F32)
    turn = iota((1, LANES), 1) // GROUP
    for g in range(bands):
        halves = []
        for h in range(2):
            block = placed[h, pl.ds(band * g, SLOT, stride=PATCH), :]
            for r in range(1, PATCH):
                block = jnp.where(
                    turn == r, placed[h, pl.ds(band * g + r, SLOT, stride=PATCH), :], block
                )
            halves.append(block)
        out_ref[pl.ds(g * 2 * SLOT, 2 * SLOT), :] = jnp.concatenate(halves, axis=0).astype(BF16)


def fold_weights(embed_ref, level_ref, query_ref, key_ref, value_ref):
    pixels, width = embed_ref.shape
    levels = level_ref.shape[0]
    ext = jnp.concatenate([embed_ref[...].astype(F32), level_ref[...]], axis=0)
    count = pixels + levels
    ext = ext - jnp.mean(ext, axis=-1, keepdims=True)
    high, low = split(ext)
    stacked = jnp.concatenate([high, low], axis=0).astype(BF16)
    keys = mul(stacked, key_ref[...])
    keys = keys[:count] + keys[count:]
    values = mul(stacked, value_ref[...])
    values = values[:count] + values[count:]
    heads = width // HEAD
    scores = None
    for q in range(LATENT):
        high_q, low_q = split(keys * query_ref[pl.ds(q, 1), :].astype(F32))
        both = jnp.concatenate([high_q, low_q], axis=0).astype(BF16)
        collect = jnp.where(
            iota((width, LANES), 1) == q * heads + iota((width, LANES), 0) // HEAD, 1.0, 0.0
        ).astype(BF16)
        part = mul(both, collect)
        part = part[:count] + part[count:]
        scores = part if scores is None else scores + part
    scores = scores * (HEAD ** (-0.5) * LOG2E)
    zeros = jnp.zeros((LANES - count, width), F32)
    high_t = jnp.concatenate([high, zeros], axis=0).astype(BF16)
    low_t = jnp.concatenate([low, zeros], axis=0).astype(BF16)
    high_b, low_b = high.astype(BF16), low.astype(BF16)
    gram = (mul_t(high_b, high_t) + (mul_t(high_b, low_t) + mul_t(low_b, high_t))) * (1.0 / width)
    row, lane = iota((count, LANES), 0), iota((count, LANES), 1)
    diagonal = jnp.sum(jnp.where(row == lane, gram, 0.0), axis=-1, keepdims=True)
    spread = jnp.where(row < pixels, gram, 2.0 * gram)
    spread = jnp.where(
        lane < pixels, spread, jnp.where((lane == pixels) & (row >= pixels), diagonal, 0.0)
    )
    folded = jnp.concatenate([values, spread, scores], axis=1)
    high_f, low_f = split(folded)
    rest = jnp.zeros((2 * LANES - 2 * count, folded.shape[1]), F32)
    return jnp.concatenate(
        [high_f[:pixels], low_f[:pixels], high_f[pixels:], low_f[pixels:], rest], axis=0
    ).astype(BF16)


def aggregate_half(rows, folded, query_ref, out_weight, levels):
    variables = rows.shape[0] // levels
    width = out_weight.shape[0]
    heads = width // HEAD
    pixels = variables * PATCH * PATCH
    grid = rows.reshape(levels, variables, SLOT, LANES)
    wide = jnp.concatenate(
        [grid[:, v].reshape(levels * SLOT, LANES) for v in range(variables)], axis=1
    )
    depth = variables * LANES
    column = iota((1, depth), 1) % GROUP // PATCH
    masked = jnp.concatenate(
        [jnp.where(column == b, wide, 0.0) for b in range(HALF)], axis=0
    ).astype(BF16)
    source, target = iota((depth, LANES), 0), iota((depth, LANES), 1)
    place = (
        source // LANES * (PATCH * PATCH) + source % LANES // GROUP * PATCH + source % PATCH
    )
    gather = jnp.where(target % pixels == place, 1.0, 0.0).astype(BF16)
    patch = mul(masked, gather)
    count = HALF * levels * SLOT
    row, lane = iota((count, LANES), 0), iota((count, LANES), 1)
    level = jnp.where(
        (lane < 2 * levels) & (lane % levels == row // SLOT % levels), 1.0, 0.0
    )
    full = jnp.concatenate([patch, level], axis=1).astype(BF16)
    product = mul(full, folded)
    values = product[:, :width]
    spread = product[:, width : width + LANES]
    scores = product[:, width + LANES :]
    variance = jnp.sum(jnp.where(lane == pixels, 1.0, patch) * spread, axis=-1, keepdims=True)
    scale = lax.rsqrt(jnp.maximum(variance, 0.0) + 1e-05)
    expo = jnp.exp2(scores * scale).reshape(HALF, levels, SLOT, LANES)
    weights = expo / jnp.sum(expo, axis=1, keepdims=True) * scale.reshape(HALF, levels, SLOT, 1)
    weights = weights.reshape(count, LANES).astype(BF16)
    mixed = []
    for q in range(LATENT):
        spread_out = jnp.where(
            iota((LANES, width), 0) == q * heads + iota((LANES, width), 1) // HEAD, 1.0, 0.0
        ).astype(BF16)
        part = mul(weights, spread_out) * values
        mixed.append(part.reshape(HALF, levels, SLOT, width).sum(axis=1).reshape(HALF * SLOT, width))
    attended = jnp.concatenate(mixed, axis=0).astype(BF16)
    latent = mul(attended, out_weight).reshape(LATENT, HALF * SLOT, width)
    latent = latent + query_ref[...].astype(F32)[:, None, :]
    return latent.astype(BF16).astype(F32)


def own_kernel(
    block_ref, embed_ref, level_ref, query_ref, key_ref, value_ref, out_w_ref, latent_ref, folded_ref
):
    folded = fold_weights(embed_ref, level_ref, query_ref, key_ref, value_ref)
    folded_ref[...] = folded
    fields = block_ref.shape[0] // (2 * SLOT)
    rows = block_ref[...].astype(F32).reshape(fields, 2, SLOT, LANES)[:, 1]
    latent_ref[...] = aggregate_half(rows, folded, query_ref, out_w_ref[...], level_ref.shape[0])


def window_kernel(
    block_ref, own_ref, folded_ref, query_ref, out_w_ref, qkv_w_ref, proj_w_ref, out_ref, slots, clean
):
    fields = block_ref.shape[0] // SLOT
    width = out_w_ref.shape[0]
    levels = fields // 4
    rows = block_ref[...].astype(F32).reshape(fields, SLOT, LANES)
    east = aggregate_half(rows, folded_ref[...], query_ref, out_w_ref[...], levels)
    half_rows = HALF * SLOT
    for q in range(LATENT):
        for c in range(width // LANES):
            part = pl.ds(c * LANES, LANES)
            slots[c, pl.ds(q * 2 * half_rows, half_rows), :] = own_ref[q, :, part]
            slots[c, pl.ds(q * 2 * half_rows + half_rows, half_rows), :] = east[
                q, :, c * LANES : (c + 1) * LANES
            ]
    for q in range(LATENT):
        for a in range(WLAT):
            for c in range(width // LANES):
                clean[pl.ds((q * WLAT + a) * WLON, WLON), pl.ds(c * LANES, LANES)] = slots[
                    c, pl.ds(q * 2 * half_rows + a, WLON, stride=SLOT), :
                ]
    members = LATENT * WLAT * WLON
    shifted = clean[...]
    center = shifted - jnp.mean(shifted, axis=-1, keepdims=True)
    spread = jnp.mean(center * center, axis=-1, keepdims=True)
    normed = (center * lax.rsqrt(spread + 1e-05)).astype(BF16)
    qkv = mul(normed, qkv_w_ref[...]).astype(BF16)
    first = iota((1, LANES), 1) < HEAD
    mixed = []
    for p in range(width // LANES):
        queries = qkv[:, p * LANES : (p + 1) * LANES]
        keys = qkv[:, width + p * LANES : width + (p + 1) * LANES]
        values = qkv[:, 2 * width + p * LANES : 2 * width + (p + 1) * LANES]
        values = jnp.concatenate(
            [values * BF16(2.0**-8), jnp.ones((members, LANES), BF16)], axis=1
        )
        found = []
        for keep in (first, jnp.logical_not(first)):
            chosen = jnp.where(keep, queries, jnp.zeros_like(queries))
            scores = mul_t(chosen, keys)
            expo = jnp.exp2(scores * (HEAD ** (-0.5) * LOG2E)).astype(BF16)
            found.append(mul(expo, values))
        both = jnp.where(jnp.concatenate([first, first], axis=1), found[0], found[1])
        mixed.append((both[:, :LANES] / both[:, LANES:] * 2.0**8).astype(BF16))
    projected = mul(jnp.concatenate(mixed, axis=1), proj_w_ref[...])
    clean[...] = shifted + projected
    for q in range(LATENT):
        for a in range(WLAT):
            out_ref[q, a] = clean[pl.ds((q * WLAT + a) * WLON, WLON), :].astype(BF16)


def whole(count):
    return [pl.BlockSpec(memory_space=pltpu.VMEM)] * count


def body(pixels, embed_weight, level_code, queries, w_key, w_value, w_out, w_qkv, w_proj):
    _, count, cols = pixels.shape
    bands = count // (PATCH * WLAT)
    width = w_out.shape[0]
    packed = pl.pallas_call(
        pack_kernel,
        out_shape=jax.ShapeDtypeStruct((bands * 2 * SLOT, LANES), BF16),
        in_specs=whole(1),
        out_specs=whole(1)[0],
        scratch_shapes=[pltpu.VMEM((2, count + 16, LANES), F32)],
        compiler_params=pltpu.CompilerParams(vmem_limit_bytes=8 * 2**20),
        cost_estimate=pl.CostEstimate(flops=8 * 10**9, bytes_accessed=2 * 10**5, transcendentals=0),
        name="pack",
    )(pixels[0].T)
    block = lax.all_to_all(
        packed.reshape(bands, 2 * SLOT, LANES), "var", split_axis=0, concat_axis=0, tiled=True
    )
    sectors = lax.axis_size("lon")
    east = lax.ppermute(block[:, :SLOT], "lon", [(i, (i - 1) % sectors) for i in range(sectors)])
    fields = block.shape[0]
    weights = (embed_weight.reshape(-1, width), level_code, queries, w_key, w_value, w_out)
    own, folded = pl.pallas_call(
        own_kernel,
        out_shape=[
            jax.ShapeDtypeStruct((LATENT, HALF * SLOT, width), F32),
            jax.ShapeDtypeStruct((2 * LANES, width + 2 * LANES), BF16),
        ],
        in_specs=whole(7),
        out_specs=whole(2),
        compiler_params=pltpu.CompilerParams(vmem_limit_bytes=24 * 2**20),
        cost_estimate=pl.CostEstimate(flops=4 * 10**9, bytes_accessed=2 * 10**6, transcendentals=0),
        name="own_half",
    )(
        block.reshape(fields * 2 * SLOT, LANES), *weights
    )
    return pl.pallas_call(
        window_kernel,
        out_shape=jax.ShapeDtypeStruct((LATENT, WLAT, WLON, width), BF16),
        in_specs=whole(7),
        out_specs=whole(1)[0],
        scratch_shapes=[
            pltpu.VMEM((width // LANES, LATENT * WLON * SLOT, LANES), F32),
            pltpu.VMEM((LATENT * WLAT * WLON, width), F32),
        ],
        compiler_params=pltpu.CompilerParams(vmem_limit_bytes=32 * 2**20),
        cost_estimate=pl.CostEstimate(flops=8 * 10**9, bytes_accessed=4 * 10**6, transcendentals=0),
        name="window",
    )(east.reshape(fields * SLOT, LANES), own, folded, queries, w_out, w_qkv, w_proj)


def solution(mesh):
    placed = (P("var", None, "lon"), P(), P(), P(), P(), P(), P(), P(), P())
    return jax.shard_map(
        body, mesh=mesh, in_specs=placed, out_specs=P(None, "var", "lon", None), check_vma=False
    )
```

```python
import jax
import jax.numpy as jnp
from jax import lax
from jax.experimental import pallas as pl
from jax.experimental.pallas import tpu as pltpu
from jax.sharding import PartitionSpec as P

HEAD = 64
LATENT = 3
WLAT = 6
WLON = 12
HALF = WLON // 2
PATCH = 4
SLOT = 8
LANES = 128
GROUP = 32
LOG2E = 1.4426950408889634
F32 = jnp.float32
BF16 = jnp.bfloat16


def mul(a, b):
    return jnp.dot(a, b, preferred_element_type=F32)


def mul_t(a, b):
    return lax.dot_general(a, b, (((1,), (1,)), ((), ())), preferred_element_type=F32)


def iota(shape, dim):
    return lax.broadcasted_iota(jnp.int32, shape, dim)


def split(value):
    high = value.astype(BF16).astype(F32)
    return high, value - high


def pack_kernel(pixel_ref, out_ref, placed):
    cols, count = pixel_ref.shape
    band = PATCH * WLAT
    bands = count // band
    source, target = iota((cols, 2 * LANES), 0), iota((cols, 2 * LANES), 1)
    place = (target // LANES == source // (cols // 2)) & (target % GROUP == source % (cols // 2))
    wide = lax.dot_general(
        pixel_ref[...],
        jnp.where(place, 1.0, 0.0).astype(BF16),
        (((0,), (0,)), ((), ())),
        preferred_element_type=F32,
    )
    for h in range(2):
        placed[h, pl.ds(0, count), :] = wide[:, h * LANES : (h + 1) * LANES]
        placed[h, pl.ds(count, 16), :] = jnp.zeros((16, LANES), F32)
    turn = iota((1, LANES), 1) // GROUP
    far = (1 - lax.axis_index("lon") % 2) * (count // 2)
    for g in range(bands):
        halves = []
        for h in range(2):
            base = band * g
            if h == 0:
                base = pl.multiple_of(far + base if g < bands // 2 else base - far, SLOT)
            block = placed[h, pl.ds(base, SLOT, stride=PATCH), :]
            for r in range(1, PATCH):
                block = jnp.where(
                    turn == r, placed[h, pl.ds(base + r, SLOT, stride=PATCH), :], block
                )
            halves.append(block)
        out_ref[pl.ds(g * 2 * SLOT, 2 * SLOT), :] = jnp.concatenate(halves, axis=0).astype(BF16)


def fold_weights(embed_ref, level_ref, query_ref, key_ref, value_ref):
    pixels, width = embed_ref.shape
    levels = level_ref.shape[0]
    ext = jnp.concatenate([embed_ref[...].astype(F32), level_ref[...]], axis=0)
    count = pixels + levels
    ext = ext - jnp.mean(ext, axis=-1, keepdims=True)
    high, low = split(ext)
    stacked = jnp.concatenate([high, low], axis=0).astype(BF16)
    keys = mul(stacked, key_ref[...])
    keys = keys[:count] + keys[count:]
    values = mul(stacked, value_ref[...])
    values = values[:count] + values[count:]
    heads = width // HEAD
    scores = None
    for q in range(LATENT):
        high_q, low_q = split(keys * query_ref[pl.ds(q, 1), :].astype(F32))
        both = jnp.concatenate([high_q, low_q], axis=0).astype(BF16)
        collect = jnp.where(
            iota((width, LANES), 1) == q * heads + iota((width, LANES), 0) // HEAD, 1.0, 0.0
        ).astype(BF16)
        part = mul(both, collect)
        part = part[:count] + part[count:]
        scores = part if scores is None else scores + part
    scores = scores * (HEAD ** (-0.5) * LOG2E)
    zeros = jnp.zeros((LANES - count, width), F32)
    high_t = jnp.concatenate([high, zeros], axis=0).astype(BF16)
    low_t = jnp.concatenate([low, zeros], axis=0).astype(BF16)
    high_b, low_b = high.astype(BF16), low.astype(BF16)
    gram = (mul_t(high_b, high_t) + (mul_t(high_b, low_t) + mul_t(low_b, high_t))) * (1.0 / width)
    row, lane = iota((count, LANES), 0), iota((count, LANES), 1)
    diagonal = jnp.sum(jnp.where(row == lane, gram, 0.0), axis=-1, keepdims=True)
    spread = jnp.where(row < pixels, gram, 2.0 * gram)
    spread = jnp.where(
        lane < pixels, spread, jnp.where((lane == pixels) & (row >= pixels), diagonal, 0.0)
    )
    folded = jnp.concatenate([values, spread, scores], axis=1)
    high_f, low_f = split(folded)
    rest = jnp.zeros((2 * LANES - 2 * count, folded.shape[1]), F32)
    return jnp.concatenate(
        [high_f[:pixels], low_f[:pixels], high_f[pixels:], low_f[pixels:], rest], axis=0
    ).astype(BF16)


def aggregate_half(rows, folded, query_ref, out_weight, levels):
    variables = rows.shape[0] // levels
    width = out_weight.shape[0]
    heads = width // HEAD
    pixels = variables * PATCH * PATCH
    grid = rows.reshape(levels, variables, SLOT, LANES)
    wide = jnp.concatenate(
        [grid[:, v].reshape(levels * SLOT, LANES) for v in range(variables)], axis=1
    )
    depth = variables * LANES
    column = iota((1, depth), 1) % GROUP // PATCH
    masked = jnp.concatenate(
        [jnp.where(column == b, wide, 0.0) for b in range(HALF)], axis=0
    ).astype(BF16)
    source, target = iota((depth, LANES), 0), iota((depth, LANES), 1)
    place = (
        source // LANES * (PATCH * PATCH) + source % LANES // GROUP * PATCH + source % PATCH
    )
    gather = jnp.where(target % pixels == place, 1.0, 0.0).astype(BF16)
    patch = mul(masked, gather)
    count = HALF * levels * SLOT
    row, lane = iota((count, LANES), 0), iota((count, LANES), 1)
    level = jnp.where(
        (lane < 2 * levels) & (lane % levels == row // SLOT % levels), 1.0, 0.0
    )
    full = jnp.concatenate([patch, level], axis=1).astype(BF16)
    product = mul(full, folded)
    values = product[:, :width]
    spread = product[:, width : width + LANES]
    scores = product[:, width + LANES :]
    variance = jnp.sum(jnp.where(lane == pixels, 1.0, patch) * spread, axis=-1, keepdims=True)
    scale = lax.rsqrt(jnp.maximum(variance, 0.0) + 1e-05)
    expo = jnp.exp2(scores * scale).reshape(HALF, levels, SLOT, LANES)
    weights = expo / jnp.sum(expo, axis=1, keepdims=True) * scale.reshape(HALF, levels, SLOT, 1)
    weights = weights.reshape(count, LANES).astype(BF16)
    mixed = []
    for q in range(LATENT):
        spread_out = jnp.where(
            iota((LANES, width), 0) == q * heads + iota((LANES, width), 1) // HEAD, 1.0, 0.0
        ).astype(BF16)
        part = mul(weights, spread_out) * values
        mixed.append(part.reshape(HALF, levels, SLOT, width).sum(axis=1).reshape(HALF * SLOT, width))
    attended = jnp.concatenate(mixed, axis=0).astype(BF16)
    latent = mul(attended, out_weight).reshape(LATENT, HALF * SLOT, width)
    latent = latent + query_ref[...].astype(F32)[:, None, :]
    return latent.astype(BF16).astype(F32)


def own_kernel(
    block_ref, embed_ref, level_ref, query_ref, key_ref, value_ref, out_w_ref, latent_ref, folded_ref
):
    folded = fold_weights(embed_ref, level_ref, query_ref, key_ref, value_ref)
    folded_ref[...] = folded
    fields = block_ref.shape[0] // (2 * SLOT)
    rows = block_ref[...].astype(F32).reshape(fields, 2, SLOT, LANES)[:, 1]
    latent_ref[...] = aggregate_half(rows, folded, query_ref, out_w_ref[...], level_ref.shape[0])


def window_kernel(
    block_ref, own_ref, folded_ref, query_ref, out_w_ref, qkv_w_ref, proj_w_ref, out_ref, slots, clean
):
    fields = block_ref.shape[0] // SLOT
    width = out_w_ref.shape[0]
    levels = fields // 4
    rows = block_ref[...].astype(F32).reshape(fields, SLOT, LANES)
    east = aggregate_half(rows, folded_ref[...], query_ref, out_w_ref[...], levels)
    half_rows = HALF * SLOT
    for q in range(LATENT):
        for c in range(width // LANES):
            part = pl.ds(c * LANES, LANES)
            slots[c, pl.ds(q * 2 * half_rows, half_rows), :] = own_ref[q, :, part]
            slots[c, pl.ds(q * 2 * half_rows + half_rows, half_rows), :] = east[
                q, :, c * LANES : (c + 1) * LANES
            ]
    for q in range(LATENT):
        for a in range(WLAT):
            for c in range(width // LANES):
                clean[pl.ds((q * WLAT + a) * WLON, WLON), pl.ds(c * LANES, LANES)] = slots[
                    c, pl.ds(q * 2 * half_rows + a, WLON, stride=SLOT), :
                ]
    members = LATENT * WLAT * WLON
    shifted = clean[...]
    center = shifted - jnp.mean(shifted, axis=-1, keepdims=True)
    spread = jnp.mean(center * center, axis=-1, keepdims=True)
    normed = (center * lax.rsqrt(spread + 1e-05)).astype(BF16)
    qkv = mul(normed, qkv_w_ref[...]).astype(BF16)
    first = iota((1, LANES), 1) < HEAD
    mixed = []
    for p in range(width // LANES):
        queries = qkv[:, p * LANES : (p + 1) * LANES]
        keys = qkv[:, width + p * LANES : width + (p + 1) * LANES]
        values = qkv[:, 2 * width + p * LANES : 2 * width + (p + 1) * LANES]
        values = jnp.concatenate(
            [values * BF16(2.0**-8), jnp.ones((members, LANES), BF16)], axis=1
        )
        found = []
        for keep in (first, jnp.logical_not(first)):
            chosen = jnp.where(keep, queries, jnp.zeros_like(queries))
            scores = mul_t(chosen, keys)
            expo = jnp.exp2(scores * (HEAD ** (-0.5) * LOG2E)).astype(BF16)
            found.append(mul(expo, values))
        both = jnp.where(jnp.concatenate([first, first], axis=1), found[0], found[1])
        mixed.append((both[:, :LANES] / both[:, LANES:] * 2.0**8).astype(BF16))
    projected = mul(jnp.concatenate(mixed, axis=1), proj_w_ref[...])
    clean[...] = shifted + projected
    for q in range(LATENT):
        for a in range(WLAT):
            out_ref[q, a] = clean[pl.ds((q * WLAT + a) * WLON, WLON), :].astype(BF16)


def whole(count):
    return [pl.BlockSpec(memory_space=pltpu.VMEM)] * count


def pack(pixels):
    _, count, _ = pixels.shape
    bands = count // (PATCH * WLAT)
    return pl.pallas_call(
        pack_kernel,
        out_shape=jax.ShapeDtypeStruct((bands * 2 * SLOT, LANES), BF16),
        in_specs=whole(1),
        out_specs=whole(1)[0],
        scratch_shapes=[pltpu.VMEM((2, count + 16, LANES), F32)],
        compiler_params=pltpu.CompilerParams(vmem_limit_bytes=8 * 2**20),
        cost_estimate=pl.CostEstimate(flops=8 * 10**9, bytes_accessed=2 * 10**5, transcendentals=0),
        name="pack",
    )(pixels[0].T)


def own_half(block, embed_weight, level_code, queries, w_key, w_value, w_out):
    width = w_out.shape[0]
    return pl.pallas_call(
        own_kernel,
        out_shape=[
            jax.ShapeDtypeStruct((LATENT, HALF * SLOT, width), F32),
            jax.ShapeDtypeStruct((2 * LANES, width + 2 * LANES), BF16),
        ],
        in_specs=whole(7),
        out_specs=whole(2),
        compiler_params=pltpu.CompilerParams(vmem_limit_bytes=24 * 2**20),
        cost_estimate=pl.CostEstimate(flops=4 * 10**9, bytes_accessed=2 * 10**6, transcendentals=0),
        name="own_half",
    )(block.reshape(-1, LANES), embed_weight.reshape(-1, width), level_code, queries, w_key, w_value, w_out)


def window(east, own, folded, queries, w_out, w_qkv, w_proj):
    width = w_out.shape[0]
    return pl.pallas_call(
        window_kernel,
        out_shape=jax.ShapeDtypeStruct((LATENT, WLAT, WLON, width), BF16),
        in_specs=whole(7),
        out_specs=whole(1)[0],
        scratch_shapes=[
            pltpu.VMEM((width // LANES, LATENT * WLON * SLOT, LANES), F32),
            pltpu.VMEM((LATENT * WLAT * WLON, width), F32),
        ],
        compiler_params=pltpu.CompilerParams(vmem_limit_bytes=32 * 2**20),
        cost_estimate=pl.CostEstimate(flops=8 * 10**9, bytes_accessed=4 * 10**6, transcendentals=0),
        name="window",
    )(east.reshape(-1, LANES), own, folded, queries, w_out, w_qkv, w_proj)


def western_pairs(bands, sectors):
    pairs = []
    for g in range(bands):
        for l in range(sectors):
            source = (g + l % 2 * (bands // 2)) % bands
            pairs.append((source * sectors + (l + 1) % sectors, g * sectors + l))
    return pairs


def body(pixels, embed_weight, level_code, queries, w_key, w_value, w_out, w_qkv, w_proj):
    packed = pack(pixels)
    bands, sectors = lax.axis_size("var"), lax.axis_size("lon")
    block = lax.all_to_all(
        packed.reshape(bands, 2 * SLOT, LANES), "var", split_axis=0, concat_axis=0, tiled=True
    )
    east = lax.ppermute(block[:, :SLOT], ("var", "lon"), western_pairs(bands, sectors))
    own, folded = own_half(block, embed_weight, level_code, queries, w_key, w_value, w_out)
    return window(east, own, folded, queries, w_out, w_qkv, w_proj)


def solution(mesh):
    placed = (P("var", None, "lon"), P(), P(), P(), P(), P(), P(), P(), P())
    return jax.shard_map(
        body, mesh=mesh, in_specs=placed, out_specs=P(None, "var", "lon", None), check_vma=False
    )
```

```python
import jax
import jax.numpy as jnp
from jax import lax
from jax.experimental import pallas as pl
from jax.experimental.pallas import tpu as pltpu
from jax.sharding import PartitionSpec as P

HEAD = 64
LATENT = 3
WLAT = 6
WLON = 12
HALF = WLON // 2
PATCH = 4
SLOT = 8
LANES = 128
GROUP = 32
HALF_ROWS = 112
LOG2E = 1.4426950408889634
F32 = jnp.float32
BF16 = jnp.bfloat16


def mul(a, b):
    return jnp.dot(a, b, preferred_element_type=F32)


def mul_t(a, b):
    return lax.dot_general(a, b, (((1,), (1,)), ((), ())), preferred_element_type=F32)


def iota(shape, dim):
    return lax.broadcasted_iota(jnp.int32, shape, dim)


def split(value):
    high = value.astype(BF16).astype(F32)
    return high, value - high


def pack_kernel(pixel_ref, out_ref, placed):
    cols, count = pixel_ref.shape
    band = PATCH * WLAT
    bands = count // band
    source, target = iota((cols, 2 * LANES), 0), iota((cols, 2 * LANES), 1)
    place = (target // LANES == source // (cols // 2)) & (target % GROUP == source % (cols // 2))
    wide = lax.dot_general(
        pixel_ref[...],
        jnp.where(place, 1.0, 0.0).astype(BF16),
        (((0,), (0,)), ((), ())),
        preferred_element_type=F32,
    )
    for h in range(2):
        placed[h, pl.ds(0, count), :] = wide[:, h * LANES : (h + 1) * LANES]
        placed[h, pl.ds(count, 16), :] = jnp.zeros((16, LANES), F32)
    turn = iota((1, LANES), 1) // GROUP
    far = (1 - lax.axis_index("lon") % 2) * (count // 2)
    for g in range(bands):
        halves = []
        for h in range(2):
            base = band * g
            if h == 0:
                base = pl.multiple_of(far + base if g < bands // 2 else base - far, SLOT)
            block = placed[h, pl.ds(base, SLOT, stride=PATCH), :]
            for r in range(1, PATCH):
                block = jnp.where(
                    turn == r, placed[h, pl.ds(base + r, SLOT, stride=PATCH), :], block
                )
            halves.append(block)
        out_ref[pl.ds(g * 2 * SLOT, 2 * SLOT), :] = jnp.concatenate(halves, axis=0).astype(BF16)


def fold_weights(embed_ref, level_ref, query_ref, key_ref, value_ref):
    pixels, width = embed_ref.shape
    levels = level_ref.shape[0]
    ext = jnp.concatenate([embed_ref[...].astype(F32), level_ref[...]], axis=0)
    count = pixels + levels
    ext = ext - jnp.mean(ext, axis=-1, keepdims=True)
    high, low = split(ext)
    stacked = jnp.concatenate([high, low], axis=0).astype(BF16)
    keys = mul(stacked, key_ref[...])
    keys = keys[:count] + keys[count:]
    values = mul(stacked, value_ref[...])
    values = values[:count] + values[count:]
    heads = width // HEAD
    scores = None
    for q in range(LATENT):
        high_q, low_q = split(keys * query_ref[pl.ds(q, 1), :].astype(F32))
        both = jnp.concatenate([high_q, low_q], axis=0).astype(BF16)
        collect = jnp.where(
            iota((width, LANES), 1) == q * heads + iota((width, LANES), 0) // HEAD, 1.0, 0.0
        ).astype(BF16)
        part = mul(both, collect)
        part = part[:count] + part[count:]
        scores = part if scores is None else scores + part
    scores = scores * (HEAD ** (-0.5) * LOG2E)
    zeros = jnp.zeros((LANES - count, width), F32)
    high_t = jnp.concatenate([high, zeros], axis=0).astype(BF16)
    low_t = jnp.concatenate([low, zeros], axis=0).astype(BF16)
    high_b, low_b = high.astype(BF16), low.astype(BF16)
    gram = (mul_t(high_b, high_t) + (mul_t(high_b, low_t) + mul_t(low_b, high_t))) * (1.0 / width)
    row, lane = iota((count, LANES), 0), iota((count, LANES), 1)
    diagonal = jnp.sum(jnp.where(row == lane, gram, 0.0), axis=-1, keepdims=True)
    spread = jnp.where(row < pixels, gram, 2.0 * gram)
    spread = jnp.where(
        lane < pixels, spread, jnp.where((lane == pixels) & (row >= pixels), diagonal, 0.0)
    )
    folded = jnp.concatenate([spread, scores, values], axis=1)
    high_f, low_f = split(folded)
    rest = jnp.zeros((2 * LANES - 2 * count, folded.shape[1]), F32)
    return jnp.concatenate(
        [high_f[:pixels], low_f[:pixels], high_f[pixels:], low_f[pixels:], rest], axis=0
    ).astype(BF16)


def constants(fields, levels, width):
    variables = fields // levels
    pixels = variables * PATCH * PATCH
    heads = width // HEAD
    depth = variables * LANES
    source, target = iota((depth, LANES), 0), iota((depth, LANES), 1)
    place = (
        source // LANES * (PATCH * PATCH) + source % LANES // GROUP * PATCH + source % PATCH
    )
    column = source % GROUP // PATCH
    gather = jnp.concatenate(
        [jnp.where((target % pixels == place) & (column == b), 1.0, 0.0) for b in range(HALF)],
        axis=1,
    ).astype(BF16)
    count = HALF * levels * SLOT
    row, lane = iota((count, LANES), 0), iota((count, LANES), 1)
    level = jnp.where(
        (lane < 2 * levels) & (lane % levels == row // SLOT % levels), 1.0, 0.0
    ).astype(BF16)
    spread = jnp.concatenate(
        [
            jnp.where(
                iota((LANES, width), 0) == q * heads + iota((LANES, width), 1) // HEAD, 1.0, 0.0
            )
            for q in range(LATENT)
        ],
        axis=1,
    ).astype(BF16)
    return gather, level, spread


def aggregate_half(rows, folded, gather, level, spread, query_ref, out_weight):
    count = level.shape[0]
    levels = count // (HALF * SLOT)
    variables = rows.shape[0] // levels
    width = out_weight.shape[0]
    pixels = variables * PATCH * PATCH
    grid = rows.reshape(levels, variables, SLOT, LANES)
    wide = jnp.concatenate(
        [grid[:, v].reshape(levels * SLOT, LANES) for v in range(variables)], axis=1
    ).astype(BF16)
    lane = iota((1, LANES), 1)
    parts = 2
    each = HALF // parts
    size = each * levels * SLOT
    patch = mul(wide, gather)
    stage = []
    for k in range(parts):
        part = jnp.concatenate(
            [patch[:, b * LANES : (b + 1) * LANES] for b in range(k * each, (k + 1) * each)], axis=0
        )
        full = jnp.concatenate([part.astype(BF16), level[:size]], axis=1)
        stage.append((part, full, mul(full, folded[:, : 2 * LANES])))
    ready = []
    for part, full, product in stage:
        moment, scores = product[:, :LANES], product[:, LANES:]
        values = mul(full, folded[:, 2 * LANES :])
        variance = jnp.sum(jnp.where(lane == pixels, 1.0, part) * moment, axis=-1, keepdims=True)
        scale = lax.rsqrt(jnp.maximum(variance, 0.0) + 1e-05)
        expo = jnp.exp2(scores * scale).reshape(each, levels, SLOT, LANES)
        weights = expo / jnp.sum(expo, axis=1, keepdims=True) * scale.reshape(each, levels, SLOT, 1)
        ready.append((weights.reshape(size, LANES).astype(BF16), values))
    pieces = [[] for _ in range(LATENT)]
    for weights, values in ready:
        for q in range(LATENT):
            part = mul(weights, spread[:, q * width : (q + 1) * width]) * values
            pieces[q].append(part.reshape(each, levels, SLOT, width).sum(axis=1).reshape(each * SLOT, width))
    mixed = [jnp.concatenate(p, axis=0) for p in pieces]
    attended = jnp.concatenate(mixed, axis=0).astype(BF16)
    latent = mul(attended, out_weight).reshape(LATENT, HALF * SLOT, width)
    latent = latent + query_ref[...].astype(F32)[:, None, :]
    return latent.astype(BF16).astype(F32)


def tokens_of(latent, slots, clean, qkv_weight):
    width = latent.shape[-1]
    for c in range(width // LANES):
        slots[c] = latent[:, :, c * LANES : (c + 1) * LANES].reshape(slots.shape[1:])
    pairs = LATENT * WLAT
    for q in range(LATENT):
        for a in range(WLAT):
            for c in range(width // LANES):
                clean[pl.ds((q * WLAT + a) * HALF, HALF), pl.ds(c * LANES, LANES)] = slots[
                    c, pl.ds(q * HALF * SLOT + a, HALF, stride=SLOT), :
                ]
    clean[pl.ds(pairs * HALF, HALF_ROWS - pairs * HALF), :] = jnp.zeros(
        (HALF_ROWS - pairs * HALF, width), F32
    )
    shifted = clean[...]
    center = shifted - jnp.mean(shifted, axis=-1, keepdims=True)
    spread = jnp.mean(center * center, axis=-1, keepdims=True)
    normed = (center * lax.rsqrt(spread + 1e-05)).astype(BF16)
    return shifted, mul(normed, qkv_weight).astype(BF16)


def own_kernel(
    block_ref, embed_ref, level_ref, query_ref, key_ref, value_ref, out_w_ref, qkv_w_ref,
    shifted_ref, qkv_ref, folded_ref, gather_ref, marks_ref, spread_ref, slots, clean,
):
    folded = fold_weights(embed_ref, level_ref, query_ref, key_ref, value_ref)
    folded_ref[...] = folded
    fields = block_ref.shape[0] // (2 * SLOT)
    gather, marks, spread = constants(fields, level_ref.shape[0], out_w_ref.shape[0])
    gather_ref[...] = gather
    marks_ref[...] = marks
    spread_ref[...] = spread
    rows = block_ref[...].astype(F32).reshape(fields, 2, SLOT, LANES)[:, 1]
    latent = aggregate_half(rows, folded, gather, marks, spread, query_ref, out_w_ref[...])
    shifted, qkv = tokens_of(latent, slots, clean, qkv_w_ref[...])
    shifted_ref[...] = shifted
    qkv_ref[...] = qkv


def window_kernel(
    block_ref, shifted_ref, qkv_ref, folded_ref, gather_ref, marks_ref, spread_ref, query_ref,
    out_w_ref, qkv_w_ref, proj_w_ref, out_ref, slots, clean, result,
):
    fields = block_ref.shape[0] // SLOT
    width = out_w_ref.shape[0]
    rows = block_ref[...].astype(F32).reshape(fields, SLOT, LANES)
    latent = aggregate_half(
        rows, folded_ref[...], gather_ref[...], marks_ref[...], spread_ref[...], query_ref, out_w_ref[...]
    )
    shifted, qkv = tokens_of(latent, slots, clean, qkv_w_ref[...])
    shifted = jnp.concatenate([shifted_ref[...], shifted], axis=0)
    qkv = jnp.concatenate([qkv_ref[...], qkv], axis=0)
    pairs = LATENT * WLAT
    row = iota((2 * HALF_ROWS, LANES), 0) % HALF_ROWS
    ones = jnp.where(row < pairs * HALF, 1.0, 0.0).astype(BF16)
    first = iota((1, LANES), 1) < HEAD
    mixed = []
    alls = []
    for p in range(width // LANES):
        queries = qkv[:, p * LANES : (p + 1) * LANES]
        keys = qkv[:, width + p * LANES : width + (p + 1) * LANES]
        values = qkv[:, 2 * width + p * LANES : 2 * width + (p + 1) * LANES]
        values = jnp.concatenate([values * BF16(2.0**-8), ones], axis=1)
        zero = jnp.zeros_like(queries)
        chosen = jnp.concatenate([jnp.where(first, queries, zero), jnp.where(first, zero, queries)], axis=0)
        scores = mul_t(chosen, keys)
        alls.append((jnp.exp2(scores * (HEAD ** (-0.5) * LOG2E)).astype(BF16), values))
    for expo, values in alls:
        found = mul(expo, values).reshape(2, 2 * HALF_ROWS, 2 * LANES)
        both = jnp.where(jnp.concatenate([first, first], axis=1), found[0], found[1])
        mixed.append((both[:, :LANES] / both[:, LANES:] * 2.0**8).astype(BF16))
    result[...] = shifted + mul(jnp.concatenate(mixed, axis=1), proj_w_ref[...])
    for i in range(pairs):
        out_ref[i // WLAT, i % WLAT] = jnp.concatenate(
            [result[pl.ds(i * HALF, HALF), :], result[pl.ds(HALF_ROWS + i * HALF, HALF), :]], axis=0
        ).astype(BF16)


def whole(count):
    return [pl.BlockSpec(memory_space=pltpu.VMEM)] * count


def pack(pixels):
    _, count, _ = pixels.shape
    bands = count // (PATCH * WLAT)
    return pl.pallas_call(
        pack_kernel,
        out_shape=jax.ShapeDtypeStruct((bands * 2 * SLOT, LANES), BF16),
        in_specs=whole(1),
        out_specs=whole(1)[0],
        scratch_shapes=[pltpu.VMEM((2, count + 16, LANES), F32)],
        compiler_params=pltpu.CompilerParams(vmem_limit_bytes=8 * 2**20),
        cost_estimate=pl.CostEstimate(flops=8 * 10**9, bytes_accessed=2 * 10**5, transcendentals=0),
        name="pack",
    )(pixels[0].T)


def scratch(width):
    return [
        pltpu.VMEM((width // LANES, LATENT * HALF * SLOT, LANES), F32),
        pltpu.VMEM((HALF_ROWS, width), F32),
    ]


def own_half(block, embed_weight, level_code, queries, w_key, w_value, w_out, w_qkv):
    width = w_out.shape[0]
    fields, levels = block.shape[0], level_code.shape[0]
    return pl.pallas_call(
        own_kernel,
        out_shape=[
            jax.ShapeDtypeStruct((HALF_ROWS, width), F32),
            jax.ShapeDtypeStruct((HALF_ROWS, w_qkv.shape[1]), BF16),
            jax.ShapeDtypeStruct((2 * LANES, width + 2 * LANES), BF16),
            jax.ShapeDtypeStruct((fields // levels * LANES, HALF * LANES), BF16),
            jax.ShapeDtypeStruct((HALF * levels * SLOT, LANES), BF16),
            jax.ShapeDtypeStruct((LANES, LATENT * width), BF16),
        ],
        in_specs=whole(8),
        out_specs=whole(6),
        scratch_shapes=scratch(width),
        compiler_params=pltpu.CompilerParams(vmem_limit_bytes=24 * 2**20),
        cost_estimate=pl.CostEstimate(flops=4 * 10**9, bytes_accessed=2 * 10**6, transcendentals=0),
        name="own_half",
    )(
        block.reshape(-1, LANES), embed_weight.reshape(-1, width), level_code, queries, w_key, w_value,
        w_out, w_qkv,
    )


def window(east, own, queries, w_out, w_qkv, w_proj):
    width = w_out.shape[0]
    return pl.pallas_call(
        window_kernel,
        out_shape=jax.ShapeDtypeStruct((LATENT, WLAT, WLON, width), BF16),
        in_specs=whole(11),
        out_specs=whole(1)[0],
        scratch_shapes=scratch(width) + [pltpu.VMEM((2 * HALF_ROWS, width), F32)],
        compiler_params=pltpu.CompilerParams(vmem_limit_bytes=32 * 2**20),
        cost_estimate=pl.CostEstimate(flops=8 * 10**9, bytes_accessed=4 * 10**6, transcendentals=0),
        name="window",
    )(east.reshape(-1, LANES), *own, queries, w_out, w_qkv, w_proj)


def western_pairs(bands, sectors):
    pairs = []
    for g in range(bands):
        for l in range(sectors):
            source = (g + l % 2 * (bands // 2)) % bands
            pairs.append((source * sectors + (l + 1) % sectors, g * sectors + l))
    return pairs


def body(pixels, embed_weight, level_code, queries, w_key, w_value, w_out, w_qkv, w_proj):
    packed = pack(pixels)
    bands, sectors = lax.axis_size("var"), lax.axis_size("lon")
    block = lax.all_to_all(
        packed.reshape(bands, 2 * SLOT, LANES), "var", split_axis=0, concat_axis=0, tiled=True
    )
    east = lax.ppermute(block[:, :SLOT], ("var", "lon"), western_pairs(bands, sectors))
    own = own_half(block, embed_weight, level_code, queries, w_key, w_value, w_out, w_qkv)
    return window(east, own, queries, w_out, w_qkv, w_proj)


def solution(mesh):
    placed = (P("var", None, "lon"), P(), P(), P(), P(), P(), P(), P(), P())
    return jax.shard_map(
        body, mesh=mesh, in_specs=placed, out_specs=P(None, "var", "lon", None), check_vma=False
    )
```

```python
import jax
import jax.numpy as jnp
from jax import lax
from jax.experimental import pallas as pl
from jax.experimental.pallas import tpu as pltpu
from jax.sharding import PartitionSpec as P

HEAD = 64
LATENT = 3
WLAT = 6
WLON = 12
HALF = WLON // 2
PATCH = 4
SLOT = 8
LANES = 128
GROUP = 32
HALF_ROWS = 112
LOG2E = 1.4426950408889634
F32 = jnp.float32
BF16 = jnp.bfloat16


def mul(a, b):
    return jnp.dot(a, b, preferred_element_type=F32)


def mul_t(a, b):
    return lax.dot_general(a, b, (((1,), (1,)), ((), ())), preferred_element_type=F32)


def iota(shape, dim):
    return lax.broadcasted_iota(jnp.int32, shape, dim)


def split(value):
    high = value.astype(BF16).astype(F32)
    return high, value - high


def pack_kernel(pixel_ref, out_ref, placed):
    cols, count = pixel_ref.shape
    band = PATCH * WLAT
    bands = count // band
    source, target = iota((cols, 2 * LANES), 0), iota((cols, 2 * LANES), 1)
    place = (target // LANES == source // (cols // 2)) & (target % GROUP == source % (cols // 2))
    wide = lax.dot_general(
        pixel_ref[...],
        jnp.where(place, 1.0, 0.0).astype(BF16),
        (((0,), (0,)), ((), ())),
        preferred_element_type=F32,
    )
    for h in range(2):
        placed[h, pl.ds(0, count), :] = wide[:, h * LANES : (h + 1) * LANES]
        placed[h, pl.ds(count, 16), :] = jnp.zeros((16, LANES), F32)
    turn = iota((1, LANES), 1) // GROUP
    far = (1 - lax.axis_index("lon") % 2) * (count // 2)
    for g in range(bands):
        halves = []
        for h in range(2):
            base = band * g
            if h == 0:
                base = pl.multiple_of(far + base if g < bands // 2 else base - far, SLOT)
            block = placed[h, pl.ds(base, SLOT, stride=PATCH), :]
            for r in range(1, PATCH):
                block = jnp.where(
                    turn == r, placed[h, pl.ds(base + r, SLOT, stride=PATCH), :], block
                )
            halves.append(block)
        out_ref[pl.ds(g * 2 * SLOT, 2 * SLOT), :] = jnp.concatenate(halves, axis=0).astype(BF16)


def fold_weights(embed_ref, level_ref, query_ref, key_ref, value_ref):
    pixels, width = embed_ref.shape
    levels = level_ref.shape[0]
    ext = jnp.concatenate([embed_ref[...].astype(F32), level_ref[...]], axis=0)
    count = pixels + levels
    ext = ext - jnp.mean(ext, axis=-1, keepdims=True)
    high, low = split(ext)
    stacked = jnp.concatenate([high, low], axis=0).astype(BF16)
    keys = mul(stacked, key_ref[...])
    keys = keys[:count] + keys[count:]
    values = mul(stacked, value_ref[...])
    values = values[:count] + values[count:]
    heads = width // HEAD
    scores = None
    for q in range(LATENT):
        high_q, low_q = split(keys * query_ref[pl.ds(q, 1), :].astype(F32))
        both = jnp.concatenate([high_q, low_q], axis=0).astype(BF16)
        collect = jnp.where(
            iota((width, LANES), 1) == q * heads + iota((width, LANES), 0) // HEAD, 1.0, 0.0
        ).astype(BF16)
        part = mul(both, collect)
        part = part[:count] + part[count:]
        scores = part if scores is None else scores + part
    scores = scores * (HEAD ** (-0.5) * LOG2E)
    zeros = jnp.zeros((LANES - count, width), F32)
    high_t = jnp.concatenate([high, zeros], axis=0).astype(BF16)
    low_t = jnp.concatenate([low, zeros], axis=0).astype(BF16)
    high_b, low_b = high.astype(BF16), low.astype(BF16)
    gram = (mul_t(high_b, high_t) + (mul_t(high_b, low_t) + mul_t(low_b, high_t))) * (1.0 / width)
    row, lane = iota((count, LANES), 0), iota((count, LANES), 1)
    diagonal = jnp.sum(jnp.where(row == lane, gram, 0.0), axis=-1, keepdims=True)
    spread = jnp.where(row < pixels, gram, 2.0 * gram)
    spread = jnp.where(
        lane < pixels, spread, jnp.where((lane == pixels) & (row >= pixels), diagonal, 0.0)
    )
    folded = jnp.concatenate([spread, scores, values], axis=1)
    high_f, low_f = split(folded)
    rest = jnp.zeros((2 * LANES - 2 * count, folded.shape[1]), F32)
    return jnp.concatenate(
        [high_f[:pixels], low_f[:pixels], high_f[pixels:], low_f[pixels:], rest], axis=0
    ).astype(BF16)


def constants(fields, levels, width):
    variables = fields // levels
    pixels = variables * PATCH * PATCH
    heads = width // HEAD
    depth = variables * LANES
    source, target = iota((depth, LANES), 0), iota((depth, LANES), 1)
    place = (
        source // LANES * (PATCH * PATCH) + source % LANES // GROUP * PATCH + source % PATCH
    )
    column = source % GROUP // PATCH
    gather = jnp.concatenate(
        [jnp.where((target % pixels == place) & (column == b), 1.0, 0.0) for b in range(HALF)],
        axis=1,
    ).astype(BF16)
    count = HALF * levels * SLOT
    row, lane = iota((count, LANES), 0), iota((count, LANES), 1)
    level = jnp.where(
        (lane < 2 * levels) & (lane % levels == row // SLOT % levels), 1.0, 0.0
    ).astype(BF16)
    spread = jnp.concatenate(
        [
            jnp.where(
                iota((LANES, width), 0) == q * heads + iota((LANES, width), 1) // HEAD, 1.0, 0.0
            )
            for q in range(LATENT)
        ],
        axis=1,
    ).astype(BF16)
    return gather, level, spread


def aggregate_half(rows, folded, gather, level, spread):
    count = level.shape[0]
    levels = count // (HALF * SLOT)
    variables = rows.shape[0] // levels
    width = spread.shape[1] // LATENT
    pixels = variables * PATCH * PATCH
    grid = rows.reshape(levels, variables, SLOT, LANES)
    wide = jnp.concatenate(
        [grid[:, v].reshape(levels * SLOT, LANES) for v in range(variables)], axis=1
    ).astype(BF16)
    lane = iota((1, LANES), 1)
    parts = 2
    each = HALF // parts
    size = each * levels * SLOT
    patch = mul(wide, gather)
    stage = []
    for k in range(parts):
        part = jnp.concatenate(
            [patch[:, b * LANES : (b + 1) * LANES] for b in range(k * each, (k + 1) * each)], axis=0
        )
        full = jnp.concatenate([part.astype(BF16), level[:size]], axis=1)
        stage.append((part, full, mul(full, folded[:, : 2 * LANES])))
    ready = []
    for part, full, product in stage:
        moment, scores = product[:, :LANES], product[:, LANES:]
        values = mul(full, folded[:, 2 * LANES :])
        variance = jnp.sum(jnp.where(lane == pixels, 1.0, part) * moment, axis=-1, keepdims=True)
        scale = lax.rsqrt(jnp.maximum(variance, 0.0) + 1e-05)
        expo = jnp.exp2(scores * scale).reshape(each, levels, SLOT, LANES)
        weights = expo / jnp.sum(expo, axis=1, keepdims=True) * scale.reshape(each, levels, SLOT, 1)
        ready.append((weights.reshape(size, LANES).astype(BF16), values))
    pieces = [[] for _ in range(LATENT)]
    for weights, values in ready:
        for q in range(LATENT):
            part = mul(weights, spread[:, q * width : (q + 1) * width]) * values
            pieces[q].append(part.reshape(each, levels, SLOT, width).sum(axis=1).reshape(each * SLOT, width))
    mixed = [jnp.concatenate(p, axis=0) for p in pieces]
    return jnp.concatenate(mixed, axis=0)


def fold_window(query_ref, out_weight, qkv_weight):
    weight = out_weight.astype(F32)
    weight = weight - jnp.mean(weight, axis=-1, keepdims=True)
    through = mul(weight.astype(BF16), qkv_weight).astype(BF16)
    queries = query_ref[...].astype(F32)
    high, low = split(queries - jnp.mean(queries, axis=-1, keepdims=True))
    rest = jnp.zeros((16 - 2 * LATENT, queries.shape[1]), F32)
    base = mul(jnp.concatenate([high, low, rest], axis=0).astype(BF16), qkv_weight)
    base = base[:LATENT] + base[LATENT : 2 * LATENT]

    def by_token(value):
        latent = iota((HALF_ROWS, value.shape[1]), 0) // (WLAT * HALF)
        rows = jnp.zeros(latent.shape, F32)
        for q in range(LATENT):
            rows = jnp.where(latent == q, value[q : q + 1], rows)
        return rows

    return through, by_token(base), by_token(queries)


def tokens_of(attended, slots, clean, out_weight, through, base, queries):
    width = attended.shape[1]
    for c in range(width // LANES):
        slots[c] = attended[:, c * LANES : (c + 1) * LANES]
    pairs = LATENT * WLAT
    for q in range(LATENT):
        for a in range(WLAT):
            for c in range(width // LANES):
                clean[pl.ds((q * WLAT + a) * HALF, HALF), pl.ds(c * LANES, LANES)] = slots[
                    c, pl.ds(q * HALF * SLOT + a, HALF, stride=SLOT), :
                ]
    clean[pl.ds(pairs * HALF, HALF_ROWS - pairs * HALF), :] = jnp.zeros(
        (HALF_ROWS - pairs * HALF, width), F32
    )
    tokens = clean[...].astype(BF16)
    shifted = (mul(tokens, out_weight) + queries).astype(BF16).astype(F32)
    qkv = mul(tokens, through) + base
    center = shifted - jnp.mean(shifted, axis=-1, keepdims=True)
    spread = jnp.mean(center * center, axis=-1, keepdims=True)
    return shifted, (qkv * lax.rsqrt(spread + 1e-05)).astype(BF16)


def own_kernel(
    block_ref, embed_ref, level_ref, query_ref, key_ref, value_ref, out_w_ref, qkv_w_ref,
    shifted_ref, qkv_ref, folded_ref, gather_ref, marks_ref, spread_ref, through_ref, base_ref,
    rows_ref, slots, clean,
):
    folded = fold_weights(embed_ref, level_ref, query_ref, key_ref, value_ref)
    folded_ref[...] = folded
    fields = block_ref.shape[0] // (2 * SLOT)
    gather, marks, spread = constants(fields, level_ref.shape[0], out_w_ref.shape[0])
    gather_ref[...] = gather
    marks_ref[...] = marks
    spread_ref[...] = spread
    through, base, queries = fold_window(query_ref, out_w_ref[...], qkv_w_ref[...])
    through_ref[...] = through
    base_ref[...] = base
    rows_ref[...] = queries
    rows = block_ref[...].astype(F32).reshape(fields, 2, SLOT, LANES)[:, 1]
    attended = aggregate_half(rows, folded, gather, marks, spread)
    shifted, qkv = tokens_of(attended, slots, clean, out_w_ref[...], through, base, queries)
    shifted_ref[...] = shifted
    qkv_ref[...] = qkv


def window_kernel(
    block_ref, shifted_ref, qkv_ref, folded_ref, gather_ref, marks_ref, spread_ref, through_ref,
    base_ref, rows_ref, out_w_ref, proj_w_ref, out_ref, slots, clean, result,
):
    fields = block_ref.shape[0] // SLOT
    width = out_w_ref.shape[0]
    rows = block_ref[...].astype(F32).reshape(fields, SLOT, LANES)
    attended = aggregate_half(rows, folded_ref[...], gather_ref[...], marks_ref[...], spread_ref[...])
    shifted, qkv = tokens_of(
        attended, slots, clean, out_w_ref[...], through_ref[...], base_ref[...], rows_ref[...]
    )
    shifted = jnp.concatenate([shifted_ref[...], shifted], axis=0)
    qkv = jnp.concatenate([qkv_ref[...], qkv], axis=0)
    pairs = LATENT * WLAT
    row = iota((2 * HALF_ROWS, LANES), 0) % HALF_ROWS
    ones = jnp.where(row < pairs * HALF, 1.0, 0.0).astype(BF16)
    first = iota((1, LANES), 1) < HEAD
    mixed = []
    alls = []
    for p in range(width // LANES):
        queries = qkv[:, p * LANES : (p + 1) * LANES]
        keys = qkv[:, width + p * LANES : width + (p + 1) * LANES]
        values = qkv[:, 2 * width + p * LANES : 2 * width + (p + 1) * LANES]
        values = jnp.concatenate([values * BF16(2.0**-8), ones], axis=1)
        zero = jnp.zeros_like(queries)
        chosen = jnp.concatenate([jnp.where(first, queries, zero), jnp.where(first, zero, queries)], axis=0)
        scores = mul_t(chosen, keys)
        alls.append((jnp.exp2(scores * (HEAD ** (-0.5) * LOG2E)).astype(BF16), values))
    for expo, values in alls:
        found = mul(expo, values).reshape(2, 2 * HALF_ROWS, 2 * LANES)
        both = jnp.where(jnp.concatenate([first, first], axis=1), found[0], found[1])
        mixed.append((both[:, :LANES] / both[:, LANES:] * 2.0**8).astype(BF16))
    result[...] = shifted + mul(jnp.concatenate(mixed, axis=1), proj_w_ref[...])
    for i in range(pairs):
        out_ref[i // WLAT, i % WLAT] = jnp.concatenate(
            [result[pl.ds(i * HALF, HALF), :], result[pl.ds(HALF_ROWS + i * HALF, HALF), :]], axis=0
        ).astype(BF16)


def whole(count):
    return [pl.BlockSpec(memory_space=pltpu.VMEM)] * count


def pack(pixels):
    _, count, _ = pixels.shape
    bands = count // (PATCH * WLAT)
    return pl.pallas_call(
        pack_kernel,
        out_shape=jax.ShapeDtypeStruct((bands * 2 * SLOT, LANES), BF16),
        in_specs=whole(1),
        out_specs=whole(1)[0],
        scratch_shapes=[pltpu.VMEM((2, count + 16, LANES), F32)],
        compiler_params=pltpu.CompilerParams(vmem_limit_bytes=8 * 2**20),
        cost_estimate=pl.CostEstimate(flops=8 * 10**9, bytes_accessed=2 * 10**5, transcendentals=0),
        name="pack",
    )(pixels[0].T)


def scratch(width):
    return [
        pltpu.VMEM((width // LANES, LATENT * HALF * SLOT, LANES), F32),
        pltpu.VMEM((HALF_ROWS, width), F32),
    ]


def own_half(block, embed_weight, level_code, queries, w_key, w_value, w_out, w_qkv):
    width = w_out.shape[0]
    fields, levels = block.shape[0], level_code.shape[0]
    return pl.pallas_call(
        own_kernel,
        out_shape=[
            jax.ShapeDtypeStruct((HALF_ROWS, width), F32),
            jax.ShapeDtypeStruct((HALF_ROWS, w_qkv.shape[1]), BF16),
            jax.ShapeDtypeStruct((2 * LANES, width + 2 * LANES), BF16),
            jax.ShapeDtypeStruct((fields // levels * LANES, HALF * LANES), BF16),
            jax.ShapeDtypeStruct((HALF * levels * SLOT, LANES), BF16),
            jax.ShapeDtypeStruct((LANES, LATENT * width), BF16),
            jax.ShapeDtypeStruct(w_qkv.shape, BF16),
            jax.ShapeDtypeStruct((HALF_ROWS, w_qkv.shape[1]), F32),
            jax.ShapeDtypeStruct((HALF_ROWS, width), F32),
        ],
        in_specs=whole(8),
        out_specs=whole(9),
        scratch_shapes=scratch(width),
        compiler_params=pltpu.CompilerParams(vmem_limit_bytes=24 * 2**20),
        cost_estimate=pl.CostEstimate(flops=4 * 10**9, bytes_accessed=2 * 10**6, transcendentals=0),
        name="own_half",
    )(
        block.reshape(-1, LANES), embed_weight.reshape(-1, width), level_code, queries, w_key, w_value,
        w_out, w_qkv,
    )


def window(east, own, w_out, w_proj):
    width = w_out.shape[0]
    return pl.pallas_call(
        window_kernel,
        out_shape=jax.ShapeDtypeStruct((LATENT, WLAT, WLON, width), BF16),
        in_specs=whole(12),
        out_specs=whole(1)[0],
        scratch_shapes=scratch(width) + [pltpu.VMEM((2 * HALF_ROWS, width), F32)],
        compiler_params=pltpu.CompilerParams(vmem_limit_bytes=32 * 2**20),
        cost_estimate=pl.CostEstimate(flops=8 * 10**9, bytes_accessed=4 * 10**6, transcendentals=0),
        name="window",
    )(east.reshape(-1, LANES), *own, w_out, w_proj)


def western_pairs(bands, sectors):
    pairs = []
    for g in range(bands):
        for l in range(sectors):
            source = (g + l % 2 * (bands // 2)) % bands
            pairs.append((source * sectors + (l + 1) % sectors, g * sectors + l))
    return pairs


def body(pixels, embed_weight, level_code, queries, w_key, w_value, w_out, w_qkv, w_proj):
    packed = pack(pixels)
    bands, sectors = lax.axis_size("var"), lax.axis_size("lon")
    block = lax.all_to_all(
        packed.reshape(bands, 2 * SLOT, LANES), "var", split_axis=0, concat_axis=0, tiled=True
    )
    east = lax.ppermute(block[:, :SLOT], ("var", "lon"), western_pairs(bands, sectors))
    own = own_half(block, embed_weight, level_code, queries, w_key, w_value, w_out, w_qkv)
    return window(east, own, w_out, w_proj)


def solution(mesh):
    placed = (P("var", None, "lon"), P(), P(), P(), P(), P(), P(), P(), P())
    return jax.shard_map(
        body, mesh=mesh, in_specs=placed, out_specs=P(None, "var", "lon", None), check_vma=False
    )
```

```python
import jax
import jax.numpy as jnp
from jax import lax
from jax.experimental import pallas as pl
from jax.experimental.pallas import tpu as pltpu
from jax.sharding import PartitionSpec as P

HEAD = 64
LATENT = 3
WLAT = 6
WLON = 12
HALF = WLON // 2
PATCH = 4
SLOT = 8
LANES = 128
GROUP = 32
HALF_ROWS = 112
LOG2E = 1.4426950408889634
F32 = jnp.float32
BF16 = jnp.bfloat16


def member_order(members, depth=8):
    far = [g for g in reversed(range(members)) if g % depth >= depth // 2]
    near = sorted(
        (g for g in range(members) if g % depth < depth // 2), key=lambda g: (g % depth, g), reverse=True
    )
    first = far.index(members // 2 + depth - 2)
    far[0], far[first] = far[first], far[0]
    return [g for pair in zip(far, near) for g in pair]


def mul(a, b):
    return jnp.dot(a, b, preferred_element_type=F32)


def mul_t(a, b):
    return lax.dot_general(a, b, (((1,), (1,)), ((), ())), preferred_element_type=F32)


def iota(shape, dim):
    return lax.broadcasted_iota(jnp.int32, shape, dim)


def split(value):
    high = value.astype(BF16).astype(F32)
    return high, value - high


def pack_kernel(pixel_ref, out_ref, placed):
    cols, count = pixel_ref.shape
    band = PATCH * WLAT
    bands = count // band
    source, target = iota((cols, 2 * LANES), 0), iota((cols, 2 * LANES), 1)
    place = (target // LANES == source // (cols // 2)) & (target % GROUP == source % (cols // 2))
    wide = lax.dot_general(
        pixel_ref[...],
        jnp.where(place, 1.0, 0.0).astype(BF16),
        (((0,), (0,)), ((), ())),
        preferred_element_type=F32,
    )
    for h in range(2):
        placed[h, pl.ds(0, count), :] = wide[:, h * LANES : (h + 1) * LANES]
        placed[h, pl.ds(count, 16), :] = jnp.zeros((16, LANES), F32)
    turn = iota((1, LANES), 1) // GROUP
    far = (1 - lax.axis_index("lon") % 2) * (count // 2)
    for place_at, g in enumerate(member_order(bands)):
        halves = []
        for h in range(2):
            base = band * g
            if h == 0:
                base = pl.multiple_of(far + base if g < bands // 2 else base - far, SLOT)
            block = placed[h, pl.ds(base, SLOT, stride=PATCH), :]
            for r in range(1, PATCH):
                block = jnp.where(
                    turn == r, placed[h, pl.ds(base + r, SLOT, stride=PATCH), :], block
                )
            halves.append(block)
        out_ref[pl.ds(place_at * 2 * SLOT, 2 * SLOT), :] = jnp.concatenate(halves, axis=0).astype(BF16)


def fold_weights(embed_ref, level_ref, query_ref, key_ref, value_ref):
    pixels, width = embed_ref.shape
    levels = level_ref.shape[0]
    ext = jnp.concatenate([embed_ref[...].astype(F32), level_ref[...]], axis=0)
    count = pixels + levels
    ext = ext - jnp.mean(ext, axis=-1, keepdims=True)
    high, low = split(ext)
    stacked = jnp.concatenate([high, low], axis=0).astype(BF16)
    keys = mul(stacked, key_ref[...])
    keys = keys[:count] + keys[count:]
    values = mul(stacked, value_ref[...])
    values = values[:count] + values[count:]
    heads = width // HEAD
    scores = None
    for q in range(LATENT):
        high_q, low_q = split(keys * query_ref[pl.ds(q, 1), :].astype(F32))
        both = jnp.concatenate([high_q, low_q], axis=0).astype(BF16)
        collect = jnp.where(
            iota((width, LANES), 1) == q * heads + iota((width, LANES), 0) // HEAD, 1.0, 0.0
        ).astype(BF16)
        part = mul(both, collect)
        part = part[:count] + part[count:]
        scores = part if scores is None else scores + part
    scores = scores * (HEAD ** (-0.5) * LOG2E)
    zeros = jnp.zeros((LANES - count, width), F32)
    high_t = jnp.concatenate([high, zeros], axis=0).astype(BF16)
    low_t = jnp.concatenate([low, zeros], axis=0).astype(BF16)
    high_b, low_b = high.astype(BF16), low.astype(BF16)
    gram = (mul_t(high_b, high_t) + (mul_t(high_b, low_t) + mul_t(low_b, high_t))) * (1.0 / width)
    row, lane = iota((count, LANES), 0), iota((count, LANES), 1)
    diagonal = jnp.sum(jnp.where(row == lane, gram, 0.0), axis=-1, keepdims=True)
    spread = jnp.where(row < pixels, gram, 2.0 * gram)
    spread = jnp.where(
        lane < pixels, spread, jnp.where((lane == pixels) & (row >= pixels), diagonal, 0.0)
    )
    folded = jnp.concatenate([spread, scores, values], axis=1)
    high_f, low_f = split(folded)
    rest = jnp.zeros((2 * LANES - 2 * count, folded.shape[1]), F32)
    return jnp.concatenate(
        [high_f[:pixels], low_f[:pixels], high_f[pixels:], low_f[pixels:], rest], axis=0
    ).astype(BF16)


def constants(fields, levels, width):
    variables = fields // levels
    pixels = variables * PATCH * PATCH
    heads = width // HEAD
    depth = variables * LANES
    source, target = iota((depth, LANES), 0), iota((depth, LANES), 1)
    place = (
        source // LANES * (PATCH * PATCH) + source % LANES // GROUP * PATCH + source % PATCH
    )
    column = source % GROUP // PATCH
    gather = jnp.concatenate(
        [jnp.where((target % pixels == place) & (column == b), 1.0, 0.0) for b in range(HALF)],
        axis=1,
    ).astype(BF16)
    count = HALF * levels * SLOT
    row, lane = iota((count, LANES), 0), iota((count, LANES), 1)
    level = jnp.where(
        (lane < 2 * levels) & (lane % levels == row // SLOT % levels), 1.0, 0.0
    ).astype(BF16)
    spread = jnp.concatenate(
        [
            jnp.where(
                iota((LANES, width), 0) == q * heads + iota((LANES, width), 1) // HEAD, 1.0, 0.0
            )
            for q in range(LATENT)
        ],
        axis=1,
    ).astype(BF16)
    return gather, level, spread


def aggregate_half(rows, folded, gather, level, spread):
    count = level.shape[0]
    levels = count // (HALF * SLOT)
    variables = rows.shape[0] // levels
    width = spread.shape[1] // LATENT
    pixels = variables * PATCH * PATCH
    order = member_order(rows.shape[0])
    wide = jnp.concatenate(
        [
            jnp.concatenate([rows[order.index(l * variables + v)] for l in range(levels)], axis=0)
            for v in range(variables)
        ],
        axis=1,
    ).astype(BF16)
    lane = iota((1, LANES), 1)
    parts = 2
    each = HALF // parts
    size = each * levels * SLOT
    patch = mul(wide, gather)
    stage = []
    for k in range(parts):
        part = jnp.concatenate(
            [patch[:, b * LANES : (b + 1) * LANES] for b in range(k * each, (k + 1) * each)], axis=0
        )
        full = jnp.concatenate([part.astype(BF16), level[:size]], axis=1)
        stage.append((part, full, mul(full, folded[:, : 2 * LANES])))
    ready = []
    for part, full, product in stage:
        moment, scores = product[:, :LANES], product[:, LANES:]
        values = mul(full, folded[:, 2 * LANES :])
        variance = jnp.sum(jnp.where(lane == pixels, 1.0, part) * moment, axis=-1, keepdims=True)
        scale = lax.rsqrt(jnp.maximum(variance, 0.0) + 1e-05)
        expo = jnp.exp2(scores * scale).reshape(each, levels, SLOT, LANES)
        weights = expo / jnp.sum(expo, axis=1, keepdims=True) * scale.reshape(each, levels, SLOT, 1)
        ready.append((weights.reshape(size, LANES).astype(BF16), values))
    pieces = [[] for _ in range(LATENT)]
    for weights, values in ready:
        for q in range(LATENT):
            part = mul(weights, spread[:, q * width : (q + 1) * width]) * values
            pieces[q].append(part.reshape(each, levels, SLOT, width).sum(axis=1).reshape(each * SLOT, width))
    mixed = [jnp.concatenate(p, axis=0) for p in pieces]
    return jnp.concatenate(mixed, axis=0)


def fold_window(query_ref, out_weight, qkv_weight):
    weight = out_weight.astype(F32)
    weight = weight - jnp.mean(weight, axis=-1, keepdims=True)
    through = mul(weight.astype(BF16), qkv_weight).astype(BF16)
    queries = query_ref[...].astype(F32)
    high, low = split(queries - jnp.mean(queries, axis=-1, keepdims=True))
    rest = jnp.zeros((16 - 2 * LATENT, queries.shape[1]), F32)
    base = mul(jnp.concatenate([high, low, rest], axis=0).astype(BF16), qkv_weight)
    base = base[:LATENT] + base[LATENT : 2 * LATENT]

    def by_token(value):
        latent = iota((HALF_ROWS, value.shape[1]), 0) // (WLAT * HALF)
        rows = jnp.zeros(latent.shape, F32)
        for q in range(LATENT):
            rows = jnp.where(latent == q, value[q : q + 1], rows)
        return rows

    return through, by_token(base), by_token(queries)


def tokens_of(attended, slots, clean, out_weight, through, base, queries):
    width = attended.shape[1]
    for c in range(width // LANES):
        slots[c] = attended[:, c * LANES : (c + 1) * LANES]
    pairs = LATENT * WLAT
    for q in range(LATENT):
        for a in range(WLAT):
            for c in range(width // LANES):
                clean[pl.ds((q * WLAT + a) * HALF, HALF), pl.ds(c * LANES, LANES)] = slots[
                    c, pl.ds(q * HALF * SLOT + a, HALF, stride=SLOT), :
                ]
    clean[pl.ds(pairs * HALF, HALF_ROWS - pairs * HALF), :] = jnp.zeros(
        (HALF_ROWS - pairs * HALF, width), F32
    )
    tokens = clean[...].astype(BF16)
    shifted = (mul(tokens, out_weight) + queries).astype(BF16).astype(F32)
    qkv = mul(tokens, through) + base
    center = shifted - jnp.mean(shifted, axis=-1, keepdims=True)
    spread = jnp.mean(center * center, axis=-1, keepdims=True)
    return shifted, (qkv * lax.rsqrt(spread + 1e-05)).astype(BF16)


def own_kernel(
    block_ref, embed_ref, level_ref, query_ref, key_ref, value_ref, out_w_ref, qkv_w_ref,
    shifted_ref, qkv_ref, folded_ref, gather_ref, marks_ref, spread_ref, through_ref, base_ref,
    rows_ref, slots, clean,
):
    folded = fold_weights(embed_ref, level_ref, query_ref, key_ref, value_ref)
    folded_ref[...] = folded
    fields = block_ref.shape[0] // (2 * SLOT)
    gather, marks, spread = constants(fields, level_ref.shape[0], out_w_ref.shape[0])
    gather_ref[...] = gather
    marks_ref[...] = marks
    spread_ref[...] = spread
    through, base, queries = fold_window(query_ref, out_w_ref[...], qkv_w_ref[...])
    through_ref[...] = through
    base_ref[...] = base
    rows_ref[...] = queries
    rows = block_ref[...].astype(F32).reshape(fields, 2, SLOT, LANES)[:, 1]
    attended = aggregate_half(rows, folded, gather, marks, spread)
    shifted, qkv = tokens_of(attended, slots, clean, out_w_ref[...], through, base, queries)
    shifted_ref[...] = shifted
    qkv_ref[...] = qkv


def window_kernel(
    block_ref, shifted_ref, qkv_ref, folded_ref, gather_ref, marks_ref, spread_ref, through_ref,
    base_ref, rows_ref, out_w_ref, proj_w_ref, out_ref, slots, clean, result,
):
    fields = block_ref.shape[0] // SLOT
    width = out_w_ref.shape[0]
    rows = block_ref[...].astype(F32).reshape(fields, SLOT, LANES)
    attended = aggregate_half(rows, folded_ref[...], gather_ref[...], marks_ref[...], spread_ref[...])
    shifted, qkv = tokens_of(
        attended, slots, clean, out_w_ref[...], through_ref[...], base_ref[...], rows_ref[...]
    )
    shifted = jnp.concatenate([shifted_ref[...], shifted], axis=0)
    qkv = jnp.concatenate([qkv_ref[...], qkv], axis=0)
    pairs = LATENT * WLAT
    row = iota((2 * HALF_ROWS, LANES), 0) % HALF_ROWS
    ones = jnp.where(row < pairs * HALF, 1.0, 0.0).astype(BF16)
    first = iota((1, LANES), 1) < HEAD
    mixed = []
    alls = []
    for p in range(width // LANES):
        queries = qkv[:, p * LANES : (p + 1) * LANES]
        keys = qkv[:, width + p * LANES : width + (p + 1) * LANES]
        values = qkv[:, 2 * width + p * LANES : 2 * width + (p + 1) * LANES]
        values = jnp.concatenate([values * BF16(2.0**-8), ones], axis=1)
        zero = jnp.zeros_like(queries)
        chosen = jnp.concatenate([jnp.where(first, queries, zero), jnp.where(first, zero, queries)], axis=0)
        scores = mul_t(chosen, keys)
        alls.append((jnp.exp2(scores * (HEAD ** (-0.5) * LOG2E)).astype(BF16), values))
    for expo, values in alls:
        found = mul(expo, values).reshape(2, 2 * HALF_ROWS, 2 * LANES)
        both = jnp.where(jnp.concatenate([first, first], axis=1), found[0], found[1])
        mixed.append((both[:, :LANES] / both[:, LANES:] * 2.0**8).astype(BF16))
    result[...] = shifted + mul(jnp.concatenate(mixed, axis=1), proj_w_ref[...])
    for i in range(pairs):
        out_ref[i // WLAT, i % WLAT] = jnp.concatenate(
            [result[pl.ds(i * HALF, HALF), :], result[pl.ds(HALF_ROWS + i * HALF, HALF), :]], axis=0
        ).astype(BF16)


def whole(count):
    return [pl.BlockSpec(memory_space=pltpu.VMEM)] * count


def pack(pixels):
    _, count, _ = pixels.shape
    bands = count // (PATCH * WLAT)
    return pl.pallas_call(
        pack_kernel,
        out_shape=jax.ShapeDtypeStruct((bands * 2 * SLOT, LANES), BF16),
        in_specs=whole(1),
        out_specs=whole(1)[0],
        scratch_shapes=[pltpu.VMEM((2, count + 16, LANES), F32)],
        compiler_params=pltpu.CompilerParams(vmem_limit_bytes=8 * 2**20),
        cost_estimate=pl.CostEstimate(flops=8 * 10**9, bytes_accessed=2 * 10**5, transcendentals=0),
        name="pack",
    )(pixels[0].T)


def scratch(width):
    return [
        pltpu.VMEM((width // LANES, LATENT * HALF * SLOT, LANES), F32),
        pltpu.VMEM((HALF_ROWS, width), F32),
    ]


def own_half(block, embed_weight, level_code, queries, w_key, w_value, w_out, w_qkv):
    width = w_out.shape[0]
    fields, levels = block.shape[0], level_code.shape[0]
    return pl.pallas_call(
        own_kernel,
        out_shape=[
            jax.ShapeDtypeStruct((HALF_ROWS, width), F32),
            jax.ShapeDtypeStruct((HALF_ROWS, w_qkv.shape[1]), BF16),
            jax.ShapeDtypeStruct((2 * LANES, width + 2 * LANES), BF16),
            jax.ShapeDtypeStruct((fields // levels * LANES, HALF * LANES), BF16),
            jax.ShapeDtypeStruct((HALF * levels * SLOT, LANES), BF16),
            jax.ShapeDtypeStruct((LANES, LATENT * width), BF16),
            jax.ShapeDtypeStruct(w_qkv.shape, BF16),
            jax.ShapeDtypeStruct((HALF_ROWS, w_qkv.shape[1]), F32),
            jax.ShapeDtypeStruct((HALF_ROWS, width), F32),
        ],
        in_specs=whole(8),
        out_specs=whole(9),
        scratch_shapes=scratch(width),
        compiler_params=pltpu.CompilerParams(vmem_limit_bytes=24 * 2**20),
        cost_estimate=pl.CostEstimate(flops=4 * 10**9, bytes_accessed=2 * 10**6, transcendentals=0),
        name="own_half",
    )(
        block.reshape(-1, LANES), embed_weight.reshape(-1, width), level_code, queries, w_key, w_value,
        w_out, w_qkv,
    )


def window(east, own, w_out, w_proj):
    width = w_out.shape[0]
    return pl.pallas_call(
        window_kernel,
        out_shape=jax.ShapeDtypeStruct((LATENT, WLAT, WLON, width), BF16),
        in_specs=whole(12),
        out_specs=whole(1)[0],
        scratch_shapes=scratch(width) + [pltpu.VMEM((2 * HALF_ROWS, width), F32)],
        compiler_params=pltpu.CompilerParams(vmem_limit_bytes=32 * 2**20),
        cost_estimate=pl.CostEstimate(flops=8 * 10**9, bytes_accessed=4 * 10**6, transcendentals=0),
        name="window",
    )(east.reshape(-1, LANES), *own, w_out, w_proj)


def western_pairs(bands, sectors):
    pairs = []
    for g in range(bands):
        for l in range(sectors):
            source = (g + l % 2 * (bands // 2)) % bands
            pairs.append((source * sectors + (l + 1) % sectors, g * sectors + l))
    return pairs


def body(pixels, embed_weight, level_code, queries, w_key, w_value, w_out, w_qkv, w_proj):
    packed = pack(pixels)
    bands, sectors = lax.axis_size("var"), lax.axis_size("lon")
    block = lax.all_to_all(
        packed.reshape(bands, 2 * SLOT, LANES),
        "var",
        split_axis=0,
        concat_axis=0,
        axis_index_groups=[member_order(bands)],
        tiled=True,
    )
    east = lax.ppermute(block[:, :SLOT], ("var", "lon"), western_pairs(bands, sectors))
    own = own_half(block, embed_weight, level_code, queries, w_key, w_value, w_out, w_qkv)
    return window(east, own, w_out, w_proj)


def solution(mesh):
    placed = (P("var", None, "lon"), P(), P(), P(), P(), P(), P(), P(), P())
    return jax.shard_map(
        body, mesh=mesh, in_specs=placed, out_specs=P(None, "var", "lon", None), check_vma=False
    )
```

```python
import jax
import jax.numpy as jnp
from jax import lax
from jax.experimental import pallas as pl
from jax.experimental.pallas import tpu as pltpu
from jax.sharding import PartitionSpec as P

HEAD = 64
LATENT = 3
WLAT = 6
WLON = 12
HALF = WLON // 2
PATCH = 4
SLOT = 8
LANES = 128
GROUP = 32
HALF_ROWS = 112
LOG2E = 1.4426950408889634
F32 = jnp.float32
BF16 = jnp.bfloat16


def member_order(members, depth=8):
    order = []
    for y in range(members // depth):
        for z in reversed(range(depth // 2)):
            order += [y * depth + depth // 2 + z, y * depth + z]
    first = order.index(2 * depth - 2)
    order[0], order[first] = order[first], order[0]
    return order


def mul(a, b):
    return jnp.dot(a, b, preferred_element_type=F32)


def mul_t(a, b):
    return lax.dot_general(a, b, (((1,), (1,)), ((), ())), preferred_element_type=F32)


def iota(shape, dim):
    return lax.broadcasted_iota(jnp.int32, shape, dim)


def split(value):
    high = value.astype(BF16).astype(F32)
    return high, value - high


def pack_kernel(pixel_ref, out_ref, placed):
    cols, count = pixel_ref.shape
    band = PATCH * WLAT
    bands = count // band
    source, target = iota((cols, 2 * LANES), 0), iota((cols, 2 * LANES), 1)
    place = (target // LANES == source // (cols // 2)) & (target % GROUP == source % (cols // 2))
    wide = lax.dot_general(
        pixel_ref[...],
        jnp.where(place, 1.0, 0.0).astype(BF16),
        (((0,), (0,)), ((), ())),
        preferred_element_type=F32,
    )
    for h in range(2):
        placed[h, pl.ds(0, count), :] = wide[:, h * LANES : (h + 1) * LANES]
        placed[h, pl.ds(count, 16), :] = jnp.zeros((16, LANES), F32)
    turn = iota((1, LANES), 1) // GROUP
    far = (1 - lax.axis_index("lon") % 2) * (count // 2)
    for place_at, g in enumerate(member_order(bands)):
        halves = []
        for h in range(2):
            base = band * g
            if h == 0:
                base = pl.multiple_of(far + base if g < bands // 2 else base - far, SLOT)
            block = placed[h, pl.ds(base, SLOT, stride=PATCH), :]
            for r in range(1, PATCH):
                block = jnp.where(
                    turn == r, placed[h, pl.ds(base + r, SLOT, stride=PATCH), :], block
                )
            halves.append(block)
        out_ref[pl.ds(place_at * 2 * SLOT, 2 * SLOT), :] = jnp.concatenate(halves, axis=0).astype(BF16)


def fold_weights(embed_ref, level_ref, query_ref, key_ref, value_ref):
    pixels, width = embed_ref.shape
    levels = level_ref.shape[0]
    ext = jnp.concatenate([embed_ref[...].astype(F32), level_ref[...]], axis=0)
    count = pixels + levels
    ext = ext - jnp.mean(ext, axis=-1, keepdims=True)
    high, low = split(ext)
    stacked = jnp.concatenate([high, low], axis=0).astype(BF16)
    keys = mul(stacked, key_ref[...])
    keys = keys[:count] + keys[count:]
    values = mul(stacked, value_ref[...])
    values = values[:count] + values[count:]
    heads = width // HEAD
    scores = None
    for q in range(LATENT):
        high_q, low_q = split(keys * query_ref[pl.ds(q, 1), :].astype(F32))
        both = jnp.concatenate([high_q, low_q], axis=0).astype(BF16)
        collect = jnp.where(
            iota((width, LANES), 1) == q * heads + iota((width, LANES), 0) // HEAD, 1.0, 0.0
        ).astype(BF16)
        part = mul(both, collect)
        part = part[:count] + part[count:]
        scores = part if scores is None else scores + part
    scores = scores * (HEAD ** (-0.5) * LOG2E)
    zeros = jnp.zeros((LANES - count, width), F32)
    high_t = jnp.concatenate([high, zeros], axis=0).astype(BF16)
    low_t = jnp.concatenate([low, zeros], axis=0).astype(BF16)
    high_b, low_b = high.astype(BF16), low.astype(BF16)
    gram = (mul_t(high_b, high_t) + (mul_t(high_b, low_t) + mul_t(low_b, high_t))) * (1.0 / width)
    row, lane = iota((count, LANES), 0), iota((count, LANES), 1)
    diagonal = jnp.sum(jnp.where(row == lane, gram, 0.0), axis=-1, keepdims=True)
    spread = jnp.where(row < pixels, gram, 2.0 * gram)
    spread = jnp.where(
        lane < pixels, spread, jnp.where((lane == pixels) & (row >= pixels), diagonal, 0.0)
    )
    folded = jnp.concatenate([spread, scores, values], axis=1)
    high_f, low_f = split(folded)
    rest = jnp.zeros((2 * LANES - 2 * count, folded.shape[1]), F32)
    return jnp.concatenate(
        [high_f[:pixels], low_f[:pixels], high_f[pixels:], low_f[pixels:], rest], axis=0
    ).astype(BF16)


def constants(fields, levels, width):
    variables = fields // levels
    pixels = variables * PATCH * PATCH
    heads = width // HEAD
    depth = variables * LANES
    source, target = iota((depth, LANES), 0), iota((depth, LANES), 1)
    place = (
        source // LANES * (PATCH * PATCH) + source % LANES // GROUP * PATCH + source % PATCH
    )
    column = source % GROUP // PATCH
    gather = jnp.concatenate(
        [jnp.where((target % pixels == place) & (column == b), 1.0, 0.0) for b in range(HALF)],
        axis=1,
    ).astype(BF16)
    count = HALF * levels * SLOT
    row, lane = iota((count, LANES), 0), iota((count, LANES), 1)
    level = jnp.where(
        (lane < 2 * levels) & (lane % levels == row // SLOT % levels), 1.0, 0.0
    ).astype(BF16)
    spread = jnp.concatenate(
        [
            jnp.where(
                iota((LANES, width), 0) == q * heads + iota((LANES, width), 1) // HEAD, 1.0, 0.0
            )
            for q in range(LATENT)
        ],
        axis=1,
    ).astype(BF16)
    return gather, level, spread


def aggregate_half(rows, folded, gather, level, spread):
    count = level.shape[0]
    levels = count // (HALF * SLOT)
    variables = rows.shape[0] // levels
    width = spread.shape[1] // LATENT
    pixels = variables * PATCH * PATCH
    order = member_order(rows.shape[0])
    wide = jnp.concatenate(
        [
            jnp.concatenate([rows[order.index(l * variables + v)] for l in range(levels)], axis=0)
            for v in range(variables)
        ],
        axis=1,
    ).astype(BF16)
    lane = iota((1, LANES), 1)
    parts = 2
    each = HALF // parts
    size = each * levels * SLOT
    patch = mul(wide, gather)
    stage = []
    for k in range(parts):
        part = jnp.concatenate(
            [patch[:, b * LANES : (b + 1) * LANES] for b in range(k * each, (k + 1) * each)], axis=0
        )
        full = jnp.concatenate([part.astype(BF16), level[:size]], axis=1)
        stage.append((part, full, mul(full, folded[:, : 2 * LANES])))
    ready = []
    for part, full, product in stage:
        moment, scores = product[:, :LANES], product[:, LANES:]
        values = mul(full, folded[:, 2 * LANES :])
        variance = jnp.sum(jnp.where(lane == pixels, 1.0, part) * moment, axis=-1, keepdims=True)
        scale = lax.rsqrt(jnp.maximum(variance, 0.0) + 1e-05)
        expo = jnp.exp2(scores * scale).reshape(each, levels, SLOT, LANES)
        weights = expo / jnp.sum(expo, axis=1, keepdims=True) * scale.reshape(each, levels, SLOT, 1)
        ready.append((weights.reshape(size, LANES).astype(BF16), values))
    pieces = [[] for _ in range(LATENT)]
    for weights, values in ready:
        for q in range(LATENT):
            part = mul(weights, spread[:, q * width : (q + 1) * width]) * values
            pieces[q].append(part.reshape(each, levels, SLOT, width).sum(axis=1).reshape(each * SLOT, width))
    mixed = [jnp.concatenate(p, axis=0) for p in pieces]
    return jnp.concatenate(mixed, axis=0)


def fold_window(query_ref, out_weight, qkv_weight):
    weight = out_weight.astype(F32)
    weight = weight - jnp.mean(weight, axis=-1, keepdims=True)
    through = mul(weight.astype(BF16), qkv_weight).astype(BF16)
    queries = query_ref[...].astype(F32)
    high, low = split(queries - jnp.mean(queries, axis=-1, keepdims=True))
    rest = jnp.zeros((16 - 2 * LATENT, queries.shape[1]), F32)
    base = mul(jnp.concatenate([high, low, rest], axis=0).astype(BF16), qkv_weight)
    base = base[:LATENT] + base[LATENT : 2 * LATENT]

    def by_token(value):
        latent = iota((HALF_ROWS, value.shape[1]), 0) // (WLAT * HALF)
        rows = jnp.zeros(latent.shape, F32)
        for q in range(LATENT):
            rows = jnp.where(latent == q, value[q : q + 1], rows)
        return rows

    return through, by_token(base), by_token(queries)


def tokens_of(attended, slots, clean, out_weight, through, base, queries):
    width = attended.shape[1]
    for c in range(width // LANES):
        slots[c] = attended[:, c * LANES : (c + 1) * LANES]
    pairs = LATENT * WLAT
    for q in range(LATENT):
        for a in range(WLAT):
            for c in range(width // LANES):
                clean[pl.ds((q * WLAT + a) * HALF, HALF), pl.ds(c * LANES, LANES)] = slots[
                    c, pl.ds(q * HALF * SLOT + a, HALF, stride=SLOT), :
                ]
    clean[pl.ds(pairs * HALF, HALF_ROWS - pairs * HALF), :] = jnp.zeros(
        (HALF_ROWS - pairs * HALF, width), F32
    )
    tokens = clean[...].astype(BF16)
    shifted = (mul(tokens, out_weight) + queries).astype(BF16).astype(F32)
    qkv = mul(tokens, through) + base
    center = shifted - jnp.mean(shifted, axis=-1, keepdims=True)
    spread = jnp.mean(center * center, axis=-1, keepdims=True)
    return shifted, (qkv * lax.rsqrt(spread + 1e-05)).astype(BF16)


def own_kernel(
    block_ref, embed_ref, level_ref, query_ref, key_ref, value_ref, out_w_ref, qkv_w_ref,
    shifted_ref, qkv_ref, folded_ref, gather_ref, marks_ref, spread_ref, through_ref, base_ref,
    rows_ref, slots, clean,
):
    folded = fold_weights(embed_ref, level_ref, query_ref, key_ref, value_ref)
    folded_ref[...] = folded
    fields = block_ref.shape[0] // (2 * SLOT)
    gather, marks, spread = constants(fields, level_ref.shape[0], out_w_ref.shape[0])
    gather_ref[...] = gather
    marks_ref[...] = marks
    spread_ref[...] = spread
    through, base, queries = fold_window(query_ref, out_w_ref[...], qkv_w_ref[...])
    through_ref[...] = through
    base_ref[...] = base
    rows_ref[...] = queries
    rows = block_ref[...].astype(F32).reshape(fields, 2, SLOT, LANES)[:, 1]
    attended = aggregate_half(rows, folded, gather, marks, spread)
    shifted, qkv = tokens_of(attended, slots, clean, out_w_ref[...], through, base, queries)
    shifted_ref[...] = shifted
    qkv_ref[...] = qkv


def window_kernel(
    block_ref, shifted_ref, qkv_ref, folded_ref, gather_ref, marks_ref, spread_ref, through_ref,
    base_ref, rows_ref, out_w_ref, proj_w_ref, out_ref, slots, clean, result,
):
    fields = block_ref.shape[0] // SLOT
    width = out_w_ref.shape[0]
    rows = block_ref[...].astype(F32).reshape(fields, SLOT, LANES)
    attended = aggregate_half(rows, folded_ref[...], gather_ref[...], marks_ref[...], spread_ref[...])
    shifted, qkv = tokens_of(
        attended, slots, clean, out_w_ref[...], through_ref[...], base_ref[...], rows_ref[...]
    )
    shifted = jnp.concatenate([shifted_ref[...], shifted], axis=0)
    qkv = jnp.concatenate([qkv_ref[...], qkv], axis=0)
    pairs = LATENT * WLAT
    row = iota((2 * HALF_ROWS, LANES), 0) % HALF_ROWS
    ones = jnp.where(row < pairs * HALF, 1.0, 0.0).astype(BF16)
    first = iota((1, LANES), 1) < HEAD
    mixed = []
    alls = []
    for p in range(width // LANES):
        queries = qkv[:, p * LANES : (p + 1) * LANES]
        keys = qkv[:, width + p * LANES : width + (p + 1) * LANES]
        values = qkv[:, 2 * width + p * LANES : 2 * width + (p + 1) * LANES]
        values = jnp.concatenate([values * BF16(2.0**-8), ones], axis=1)
        zero = jnp.zeros_like(queries)
        chosen = jnp.concatenate([jnp.where(first, queries, zero), jnp.where(first, zero, queries)], axis=0)
        scores = mul_t(chosen, keys)
        alls.append((jnp.exp2(scores * (HEAD ** (-0.5) * LOG2E)).astype(BF16), values))
    for expo, values in alls:
        found = mul(expo, values).reshape(2, 2 * HALF_ROWS, 2 * LANES)
        both = jnp.where(jnp.concatenate([first, first], axis=1), found[0], found[1])
        mixed.append((both[:, :LANES] / both[:, LANES:] * 2.0**8).astype(BF16))
    result[...] = shifted + mul(jnp.concatenate(mixed, axis=1), proj_w_ref[...])
    for i in range(pairs):
        out_ref[i // WLAT, i % WLAT] = jnp.concatenate(
            [result[pl.ds(i * HALF, HALF), :], result[pl.ds(HALF_ROWS + i * HALF, HALF), :]], axis=0
        ).astype(BF16)


def whole(count):
    return [pl.BlockSpec(memory_space=pltpu.VMEM)] * count


def pack(pixels):
    _, count, _ = pixels.shape
    bands = count // (PATCH * WLAT)
    return pl.pallas_call(
        pack_kernel,
        out_shape=jax.ShapeDtypeStruct((bands * 2 * SLOT, LANES), BF16),
        in_specs=whole(1),
        out_specs=whole(1)[0],
        scratch_shapes=[pltpu.VMEM((2, count + 16, LANES), F32)],
        compiler_params=pltpu.CompilerParams(vmem_limit_bytes=8 * 2**20),
        cost_estimate=pl.CostEstimate(flops=8 * 10**9, bytes_accessed=2 * 10**5, transcendentals=0),
        name="pack",
    )(pixels[0].T)


def scratch(width):
    return [
        pltpu.VMEM((width // LANES, LATENT * HALF * SLOT, LANES), F32),
        pltpu.VMEM((HALF_ROWS, width), F32),
    ]


def own_half(block, embed_weight, level_code, queries, w_key, w_value, w_out, w_qkv):
    width = w_out.shape[0]
    fields, levels = block.shape[0], level_code.shape[0]
    return pl.pallas_call(
        own_kernel,
        out_shape=[
            jax.ShapeDtypeStruct((HALF_ROWS, width), F32),
            jax.ShapeDtypeStruct((HALF_ROWS, w_qkv.shape[1]), BF16),
            jax.ShapeDtypeStruct((2 * LANES, width + 2 * LANES), BF16),
            jax.ShapeDtypeStruct((fields // levels * LANES, HALF * LANES), BF16),
            jax.ShapeDtypeStruct((HALF * levels * SLOT, LANES), BF16),
            jax.ShapeDtypeStruct((LANES, LATENT * width), BF16),
            jax.ShapeDtypeStruct(w_qkv.shape, BF16),
            jax.ShapeDtypeStruct((HALF_ROWS, w_qkv.shape[1]), F32),
            jax.ShapeDtypeStruct((HALF_ROWS, width), F32),
        ],
        in_specs=whole(8),
        out_specs=whole(9),
        scratch_shapes=scratch(width),
        compiler_params=pltpu.CompilerParams(vmem_limit_bytes=24 * 2**20),
        cost_estimate=pl.CostEstimate(flops=4 * 10**9, bytes_accessed=2 * 10**6, transcendentals=0),
        name="own_half",
    )(
        block.reshape(-1, LANES), embed_weight.reshape(-1, width), level_code, queries, w_key, w_value,
        w_out, w_qkv,
    )


def window(east, own, w_out, w_proj):
    width = w_out.shape[0]
    return pl.pallas_call(
        window_kernel,
        out_shape=jax.ShapeDtypeStruct((LATENT, WLAT, WLON, width), BF16),
        in_specs=whole(12),
        out_specs=whole(1)[0],
        scratch_shapes=scratch(width) + [pltpu.VMEM((2 * HALF_ROWS, width), F32)],
        compiler_params=pltpu.CompilerParams(vmem_limit_bytes=32 * 2**20),
        cost_estimate=pl.CostEstimate(flops=8 * 10**9, bytes_accessed=4 * 10**6, transcendentals=0),
        name="window",
    )(east.reshape(-1, LANES), *own, w_out, w_proj)


def western_pairs(bands, sectors):
    pairs = []
    for g in range(bands):
        for l in range(sectors):
            source = (g + l % 2 * (bands // 2)) % bands
            pairs.append((source * sectors + (l + 1) % sectors, g * sectors + l))
    return pairs


def body(pixels, embed_weight, level_code, queries, w_key, w_value, w_out, w_qkv, w_proj):
    packed = pack(pixels)
    bands, sectors = lax.axis_size("var"), lax.axis_size("lon")
    block = lax.all_to_all(
        packed.reshape(bands, 2 * SLOT, LANES),
        "var",
        split_axis=0,
        concat_axis=0,
        axis_index_groups=[member_order(bands)],
        tiled=True,
    )
    east = lax.ppermute(block[:, :SLOT], ("var", "lon"), western_pairs(bands, sectors))
    own = own_half(block, embed_weight, level_code, queries, w_key, w_value, w_out, w_qkv)
    return window(east, own, w_out, w_proj)


def solution(mesh):
    placed = (P("var", None, "lon"), P(), P(), P(), P(), P(), P(), P(), P())
    return jax.shard_map(
        body, mesh=mesh, in_specs=placed, out_specs=P(None, "var", "lon", None), check_vma=False
    )
```

```python
import jax
import jax.numpy as jnp
from jax import lax
from jax.experimental import pallas as pl
from jax.experimental.pallas import tpu as pltpu
from jax.sharding import PartitionSpec as P

HEAD = 64
LATENT = 3
WLAT = 6
WLON = 12
HALF = WLON // 2
PATCH = 4
SLOT = 8
LANES = 128
GROUP = 32
HALF_ROWS = 112
LOG2E = 1.4426950408889634
F32 = jnp.float32
BF16 = jnp.bfloat16


def member_order(members, depth=8):
    order = []
    for y in range(members // depth):
        for z in reversed(range(depth // 2)):
            order += [y * depth + depth // 2 + z, y * depth + z]
    first = order.index(2 * depth - 2)
    order[0], order[first] = order[first], order[0]
    return order


def mul(a, b):
    return jnp.dot(a, b, preferred_element_type=F32)


def mul_t(a, b):
    return lax.dot_general(a, b, (((1,), (1,)), ((), ())), preferred_element_type=F32)


def iota(shape, dim):
    return lax.broadcasted_iota(jnp.int32, shape, dim)


def split(value):
    high = value.astype(BF16).astype(F32)
    return high, value - high


def pack_kernel(pixel_ref, out_ref, placed):
    cols, count = pixel_ref.shape
    band = PATCH * WLAT
    bands = count // band
    source, target = iota((cols, 2 * LANES), 0), iota((cols, 2 * LANES), 1)
    place = (target // LANES == source // (cols // 2)) & (target % GROUP == source % (cols // 2))
    wide = lax.dot_general(
        pixel_ref[...],
        jnp.where(place, 1.0, 0.0).astype(BF16),
        (((0,), (0,)), ((), ())),
        preferred_element_type=F32,
    )
    for h in range(2):
        placed[h, pl.ds(0, count), :] = wide[:, h * LANES : (h + 1) * LANES]
        placed[h, pl.ds(count, 16), :] = jnp.zeros((16, LANES), F32)
    turn = iota((1, LANES), 1) // GROUP
    far = (1 - lax.axis_index("lon") % 2) * (count // 2)
    for place_at, g in enumerate(member_order(bands)):
        halves = []
        for h in range(2):
            base = band * g
            if h == 0:
                base = pl.multiple_of(far + base if g < bands // 2 else base - far, SLOT)
            block = placed[h, pl.ds(base, SLOT, stride=PATCH), :]
            for r in range(1, PATCH):
                block = jnp.where(
                    turn == r, placed[h, pl.ds(base + r, SLOT, stride=PATCH), :], block
                )
            halves.append(block)
        out_ref[pl.ds(place_at * 2 * SLOT, 2 * SLOT), :] = jnp.concatenate(halves, axis=0).astype(BF16)


def fold_weights(embed_ref, level_ref, query_ref, key_ref, value_ref):
    pixels, width = embed_ref.shape
    levels = level_ref.shape[0]
    ext = jnp.concatenate([embed_ref[...].astype(F32), level_ref[...]], axis=0)
    count = pixels + levels
    ext = ext - jnp.mean(ext, axis=-1, keepdims=True)
    high, low = split(ext)
    stacked = jnp.concatenate([high, low], axis=0).astype(BF16)
    keys = mul(stacked, key_ref[...])
    keys = keys[:count] + keys[count:]
    values = mul(stacked, value_ref[...])
    values = values[:count] + values[count:]
    heads = width // HEAD
    scores = None
    for q in range(LATENT):
        high_q, low_q = split(keys * query_ref[pl.ds(q, 1), :].astype(F32))
        both = jnp.concatenate([high_q, low_q], axis=0).astype(BF16)
        collect = jnp.where(
            iota((width, LANES), 1) == q * heads + iota((width, LANES), 0) // HEAD, 1.0, 0.0
        ).astype(BF16)
        part = mul(both, collect)
        part = part[:count] + part[count:]
        scores = part if scores is None else scores + part
    scores = scores * (HEAD ** (-0.5) * LOG2E)
    zeros = jnp.zeros((LANES - count, width), F32)
    high_t = jnp.concatenate([high, zeros], axis=0).astype(BF16)
    low_t = jnp.concatenate([low, zeros], axis=0).astype(BF16)
    high_b, low_b = high.astype(BF16), low.astype(BF16)
    gram = (mul_t(high_b, high_t) + (mul_t(high_b, low_t) + mul_t(low_b, high_t))) * (1.0 / width)
    row, lane = iota((count, LANES), 0), iota((count, LANES), 1)
    diagonal = jnp.sum(jnp.where(row == lane, gram, 0.0), axis=-1, keepdims=True)
    spread = jnp.where(row < pixels, gram, 2.0 * gram)
    spread = jnp.where(
        lane < pixels, spread, jnp.where((lane == pixels) & (row >= pixels), diagonal, 0.0)
    )
    folded = jnp.concatenate([spread, scores, values], axis=1)
    high_f, low_f = split(folded)
    rest = jnp.zeros((2 * LANES - 2 * count, folded.shape[1]), F32)
    return jnp.concatenate(
        [high_f[:pixels], low_f[:pixels], high_f[pixels:], low_f[pixels:], rest], axis=0
    ).astype(BF16)


def constants(fields, levels, width):
    variables = fields // levels
    pixels = variables * PATCH * PATCH
    heads = width // HEAD
    depth = variables * LANES
    source, target = iota((depth, LANES), 0), iota((depth, LANES), 1)
    place = (
        source // LANES * (PATCH * PATCH) + source % LANES // GROUP * PATCH + source % PATCH
    )
    column = source % GROUP // PATCH
    gather = jnp.concatenate(
        [jnp.where((target % pixels == place) & (column == b), 1.0, 0.0) for b in range(HALF)],
        axis=1,
    ).astype(BF16)
    count = HALF * levels * SLOT
    row, lane = iota((count, LANES), 0), iota((count, LANES), 1)
    level = jnp.where(
        (lane < 2 * levels) & (lane % levels == row // SLOT % levels), 1.0, 0.0
    ).astype(BF16)
    spread = jnp.concatenate(
        [
            jnp.where(
                iota((LANES, width), 0) == q * heads + iota((LANES, width), 1) // HEAD, 1.0, 0.0
            )
            for q in range(LATENT)
        ],
        axis=1,
    ).astype(BF16)
    return gather, level, spread


def aggregate_half(rows, folded, gather, level, spread):
    count = level.shape[0]
    levels = count // (HALF * SLOT)
    variables = rows.shape[0] // levels
    width = spread.shape[1] // LATENT
    pixels = variables * PATCH * PATCH
    order = member_order(rows.shape[0])
    wide = jnp.concatenate(
        [
            jnp.concatenate([rows[order.index(l * variables + v)] for l in range(levels)], axis=0)
            for v in range(variables)
        ],
        axis=1,
    ).astype(BF16)
    lane = iota((1, LANES), 1)
    parts = 2
    each = HALF // parts
    size = each * levels * SLOT
    patch = mul(wide, gather)
    stage = []
    for k in range(parts):
        part = jnp.concatenate(
            [patch[:, b * LANES : (b + 1) * LANES] for b in range(k * each, (k + 1) * each)], axis=0
        )
        full = jnp.concatenate([part.astype(BF16), level[:size]], axis=1)
        stage.append((part, full, mul(full, folded[:, : 2 * LANES])))
    ready = []
    for part, full, product in stage:
        moment, scores = product[:, :LANES], product[:, LANES:]
        values = mul(full, folded[:, 2 * LANES :])
        variance = jnp.sum(jnp.where(lane == pixels, 1.0, part) * moment, axis=-1, keepdims=True)
        scale = lax.rsqrt(jnp.maximum(variance, 0.0) + 1e-05)
        expo = jnp.exp2(scores * scale).reshape(each, levels, SLOT, LANES)
        weights = expo / jnp.sum(expo, axis=1, keepdims=True) * scale.reshape(each, levels, SLOT, 1)
        ready.append((weights.reshape(size, LANES).astype(BF16), values))
    pieces = [[] for _ in range(LATENT)]
    for weights, values in ready:
        for q in range(LATENT):
            part = mul(weights, spread[:, q * width : (q + 1) * width]) * values
            pieces[q].append(part.reshape(each, levels, SLOT, width).sum(axis=1).reshape(each * SLOT, width))
    mixed = [jnp.concatenate(p, axis=0) for p in pieces]
    return jnp.concatenate(mixed, axis=0)


def fold_window(query_ref, out_weight, qkv_weight):
    weight = out_weight.astype(F32)
    weight = weight - jnp.mean(weight, axis=-1, keepdims=True)
    through = mul(weight.astype(BF16), qkv_weight).astype(BF16)
    queries = query_ref[...].astype(F32)
    high, low = split(queries - jnp.mean(queries, axis=-1, keepdims=True))
    rest = jnp.zeros((16 - 2 * LATENT, queries.shape[1]), F32)
    base = mul(jnp.concatenate([high, low, rest], axis=0).astype(BF16), qkv_weight)
    base = base[:LATENT] + base[LATENT : 2 * LATENT]

    def by_token(value):
        latent = iota((HALF_ROWS, value.shape[1]), 0) // (WLAT * HALF)
        rows = jnp.zeros(latent.shape, F32)
        for q in range(LATENT):
            rows = jnp.where(latent == q, value[q : q + 1], rows)
        return rows

    return through, by_token(base), by_token(queries)


def tokens_of(attended, slots, clean, out_weight, through, base, queries):
    width = attended.shape[1]
    for c in range(width // LANES):
        slots[c, pl.ds(0, attended.shape[0]), :] = attended[:, c * LANES : (c + 1) * LANES]
    pairs = LATENT * WLAT
    for q in range(LATENT):
        for a in range(WLAT):
            for c in range(width // LANES):
                clean[pl.ds((q * WLAT + a) * HALF, HALF), pl.ds(c * LANES, LANES)] = slots[
                    c, pl.ds(q * HALF * SLOT + a, HALF, stride=SLOT), :
                ]
    clean[pl.ds(pairs * HALF, HALF_ROWS - pairs * HALF), :] = jnp.zeros(
        (HALF_ROWS - pairs * HALF, width), F32
    )
    tokens = clean[...].astype(BF16)
    shifted = (mul(tokens, out_weight) + queries).astype(BF16).astype(F32)
    qkv = mul(tokens, through) + base
    center = shifted - jnp.mean(shifted, axis=-1, keepdims=True)
    spread = jnp.mean(center * center, axis=-1, keepdims=True)
    return shifted, (qkv * lax.rsqrt(spread + 1e-05)).astype(BF16)


def own_kernel(
    block_ref, embed_ref, level_ref, query_ref, key_ref, value_ref, out_w_ref, qkv_w_ref,
    shifted_ref, qkv_ref, folded_ref, gather_ref, marks_ref, spread_ref, through_ref, base_ref,
    rows_ref, slots, clean,
):
    folded = fold_weights(embed_ref, level_ref, query_ref, key_ref, value_ref)
    folded_ref[...] = folded
    fields = block_ref.shape[0] // (2 * SLOT)
    gather, marks, spread = constants(fields, level_ref.shape[0], out_w_ref.shape[0])
    gather_ref[...] = gather
    marks_ref[...] = marks
    spread_ref[...] = spread
    through, base, queries = fold_window(query_ref, out_w_ref[...], qkv_w_ref[...])
    through_ref[...] = through
    base_ref[...] = base
    rows_ref[...] = queries
    rows = block_ref[...].astype(F32).reshape(fields, 2, SLOT, LANES)[:, 1]
    attended = aggregate_half(rows, folded, gather, marks, spread)
    shifted, qkv = tokens_of(attended, slots, clean, out_w_ref[...], through, base, queries)
    shifted_ref[...] = shifted
    qkv_ref[...] = qkv


def window_kernel(
    block_ref, shifted_ref, qkv_ref, folded_ref, gather_ref, marks_ref, spread_ref, through_ref,
    base_ref, rows_ref, out_w_ref, proj_w_ref, out_ref, slots, clean, result,
):
    fields = block_ref.shape[0] // SLOT
    width = out_w_ref.shape[0]
    rows = block_ref[...].astype(F32).reshape(fields, SLOT, LANES)
    attended = aggregate_half(rows, folded_ref[...], gather_ref[...], marks_ref[...], spread_ref[...])
    shifted, qkv = tokens_of(
        attended, slots, clean, out_w_ref[...], through_ref[...], base_ref[...], rows_ref[...]
    )
    shifted = jnp.concatenate([shifted_ref[...], shifted], axis=0)
    qkv = jnp.concatenate([qkv_ref[...], qkv], axis=0)
    pairs = LATENT * WLAT
    row = iota((2 * HALF_ROWS, LANES), 0) % HALF_ROWS
    ones = jnp.where(row < pairs * HALF, 1.0, 0.0).astype(BF16)
    first = iota((1, LANES), 1) < HEAD
    mixed = []
    alls = []
    for p in range(width // LANES):
        queries = qkv[:, p * LANES : (p + 1) * LANES]
        keys = qkv[:, width + p * LANES : width + (p + 1) * LANES]
        values = qkv[:, 2 * width + p * LANES : 2 * width + (p + 1) * LANES]
        values = jnp.concatenate([values * BF16(2.0**-8), ones], axis=1)
        zero = jnp.zeros_like(queries)
        chosen = jnp.concatenate([jnp.where(first, queries, zero), jnp.where(first, zero, queries)], axis=0)
        scores = mul_t(chosen, keys)
        alls.append((jnp.exp2(scores * (HEAD ** (-0.5) * LOG2E)).astype(BF16), values))
    for expo, values in alls:
        found = mul(expo, values).reshape(2, 2 * HALF_ROWS, 2 * LANES)
        both = jnp.where(jnp.concatenate([first, first], axis=1), found[0], found[1])
        mixed.append((both[:, :LANES] / both[:, LANES:] * 2.0**8).astype(BF16))
    result[...] = shifted + mul(jnp.concatenate(mixed, axis=1), proj_w_ref[...])
    for i in range(pairs):
        out_ref[i // WLAT, i % WLAT] = jnp.concatenate(
            [result[pl.ds(i * HALF, HALF), :], result[pl.ds(HALF_ROWS + i * HALF, HALF), :]], axis=0
        ).astype(BF16)


def whole(count):
    return [pl.BlockSpec(memory_space=pltpu.VMEM)] * count


def pack(pixels):
    _, count, _ = pixels.shape
    bands = count // (PATCH * WLAT)
    return pl.pallas_call(
        pack_kernel,
        out_shape=jax.ShapeDtypeStruct((bands * 2 * SLOT, LANES), BF16),
        in_specs=whole(1),
        out_specs=whole(1)[0],
        scratch_shapes=[pltpu.VMEM((2, count + 16, LANES), F32)],
        compiler_params=pltpu.CompilerParams(vmem_limit_bytes=8 * 2**20),
        cost_estimate=pl.CostEstimate(flops=8 * 10**9, bytes_accessed=2 * 10**5, transcendentals=0),
        name="pack",
    )(pixels[0].T)


def scratch(width):
    return [
        pltpu.VMEM((width // LANES, LATENT * HALF * SLOT + 3 * SLOT, LANES), F32),
        pltpu.VMEM((HALF_ROWS, width), F32),
    ]


def own_half(block, embed_weight, level_code, queries, w_key, w_value, w_out, w_qkv):
    width = w_out.shape[0]
    fields, levels = block.shape[0], level_code.shape[0]
    return pl.pallas_call(
        own_kernel,
        out_shape=[
            jax.ShapeDtypeStruct((HALF_ROWS, width), F32),
            jax.ShapeDtypeStruct((HALF_ROWS, w_qkv.shape[1]), BF16),
            jax.ShapeDtypeStruct((2 * LANES, width + 2 * LANES), BF16),
            jax.ShapeDtypeStruct((fields // levels * LANES, HALF * LANES), BF16),
            jax.ShapeDtypeStruct((HALF * levels * SLOT, LANES), BF16),
            jax.ShapeDtypeStruct((LANES, LATENT * width), BF16),
            jax.ShapeDtypeStruct(w_qkv.shape, BF16),
            jax.ShapeDtypeStruct((HALF_ROWS, w_qkv.shape[1]), F32),
            jax.ShapeDtypeStruct((HALF_ROWS, width), F32),
        ],
        in_specs=whole(8),
        out_specs=whole(9),
        scratch_shapes=scratch(width),
        compiler_params=pltpu.CompilerParams(vmem_limit_bytes=24 * 2**20),
        cost_estimate=pl.CostEstimate(flops=4 * 10**9, bytes_accessed=2 * 10**6, transcendentals=0),
        name="own_half",
    )(
        block.reshape(-1, LANES), embed_weight.reshape(-1, width), level_code, queries, w_key, w_value,
        w_out, w_qkv,
    )


def window(east, own, w_out, w_proj):
    width = w_out.shape[0]
    return pl.pallas_call(
        window_kernel,
        out_shape=jax.ShapeDtypeStruct((LATENT, WLAT, WLON, width), BF16),
        in_specs=whole(12),
        out_specs=whole(1)[0],
        scratch_shapes=scratch(width) + [pltpu.VMEM((2 * HALF_ROWS, width), F32)],
        compiler_params=pltpu.CompilerParams(vmem_limit_bytes=32 * 2**20),
        cost_estimate=pl.CostEstimate(flops=8 * 10**9, bytes_accessed=4 * 10**6, transcendentals=0),
        name="window",
    )(east.reshape(-1, LANES), *own, w_out, w_proj)


def western_pairs(bands, sectors):
    pairs = []
    for g in range(bands):
        for l in range(sectors):
            source = (g + l % 2 * (bands // 2)) % bands
            pairs.append((source * sectors + (l + 1) % sectors, g * sectors + l))
    return pairs


def body(pixels, embed_weight, level_code, queries, w_key, w_value, w_out, w_qkv, w_proj):
    packed = pack(pixels)
    bands, sectors = lax.axis_size("var"), lax.axis_size("lon")
    block = lax.all_to_all(
        packed.reshape(bands, 2 * SLOT, LANES),
        "var",
        split_axis=0,
        concat_axis=0,
        axis_index_groups=[member_order(bands)],
        tiled=True,
    )
    east = lax.ppermute(block[:, :SLOT], ("var", "lon"), western_pairs(bands, sectors))
    own = own_half(block, embed_weight, level_code, queries, w_key, w_value, w_out, w_qkv)
    return window(east, own, w_out, w_proj)


def solution(mesh):
    placed = (P("var", None, "lon"), P(), P(), P(), P(), P(), P(), P(), P())
    return jax.shard_map(
        body, mesh=mesh, in_specs=placed, out_specs=P(None, "var", "lon", None), check_vma=False
    )
```

```python
import jax
import jax.numpy as jnp
from jax import lax
from jax.experimental import pallas as pl
from jax.experimental.pallas import tpu as pltpu
from jax.sharding import PartitionSpec as P

HEAD = 64
LATENT = 3
WLAT = 6
WLON = 12
HALF = WLON // 2
PATCH = 4
SLOT = 8
LANES = 128
GROUP = 32
HALF_ROWS = 112
LOG2E = 1.4426950408889634
F32 = jnp.float32
BF16 = jnp.bfloat16


def member_order(members, depth=8):
    order = []
    for y in range(members // depth):
        for z in reversed(range(depth // 2)):
            order += [y * depth + depth // 2 + z, y * depth + z]
    first = order.index(2 * depth - 2)
    order[0], order[first] = order[first], order[0]
    return order


def mul(a, b):
    return jnp.dot(a, b, preferred_element_type=F32)


def mul_t(a, b):
    return lax.dot_general(a, b, (((1,), (1,)), ((), ())), preferred_element_type=F32)


def iota(shape, dim):
    return lax.broadcasted_iota(jnp.int32, shape, dim)


def split(value):
    high = value.astype(BF16).astype(F32)
    return high, value - high


def pack_kernel(pixel_ref, out_ref, placed):
    cols, count = pixel_ref.shape
    band = PATCH * WLAT
    bands = count // band
    source, target = iota((cols, 2 * LANES), 0), iota((cols, 2 * LANES), 1)
    place = (target // LANES == source // (cols // 2)) & (target % GROUP == source % (cols // 2))
    wide = lax.dot_general(
        pixel_ref[...],
        jnp.where(place, 1.0, 0.0).astype(BF16),
        (((0,), (0,)), ((), ())),
        preferred_element_type=F32,
    )
    for h in range(2):
        placed[h, pl.ds(0, count), :] = wide[:, h * LANES : (h + 1) * LANES]
        placed[h, pl.ds(count, 16), :] = jnp.zeros((16, LANES), F32)
    turn = iota((1, LANES), 1) // GROUP
    far = (1 - lax.axis_index("lon") % 2) * (count // 2)
    for place_at, g in enumerate(member_order(bands)):
        halves = []
        for h in range(2):
            base = band * g
            if h == 0:
                base = pl.multiple_of(far + base if g < bands // 2 else base - far, SLOT)
            block = placed[h, pl.ds(base, SLOT, stride=PATCH), :]
            for r in range(1, PATCH):
                block = jnp.where(
                    turn == r, placed[h, pl.ds(base + r, SLOT, stride=PATCH), :], block
                )
            halves.append(block)
        out_ref[pl.ds(place_at * 2 * SLOT, 2 * SLOT), :] = jnp.concatenate(halves, axis=0).astype(BF16)


def fold_weights(embed_ref, level_ref, query_ref, key_ref, value_ref):
    pixels, width = embed_ref.shape
    levels = level_ref.shape[0]
    ext = jnp.concatenate([embed_ref[...].astype(F32), level_ref[...]], axis=0)
    count = pixels + levels
    ext = ext - jnp.mean(ext, axis=-1, keepdims=True)
    high, low = split(ext)
    stacked = jnp.concatenate([high, low], axis=0).astype(BF16)
    keys = mul(stacked, key_ref[...])
    keys = keys[:count] + keys[count:]
    values = mul(stacked, value_ref[...])
    values = values[:count] + values[count:]
    heads = width // HEAD
    scores = None
    for q in range(LATENT):
        high_q, low_q = split(keys * query_ref[pl.ds(q, 1), :].astype(F32))
        both = jnp.concatenate([high_q, low_q], axis=0).astype(BF16)
        collect = jnp.where(
            iota((width, LANES), 1) == q * heads + iota((width, LANES), 0) // HEAD, 1.0, 0.0
        ).astype(BF16)
        part = mul(both, collect)
        part = part[:count] + part[count:]
        scores = part if scores is None else scores + part
    scores = scores * (HEAD ** (-0.5) * LOG2E)
    zeros = jnp.zeros((LANES - count, width), F32)
    high_t = jnp.concatenate([high, zeros], axis=0).astype(BF16)
    low_t = jnp.concatenate([low, zeros], axis=0).astype(BF16)
    high_b, low_b = high.astype(BF16), low.astype(BF16)
    gram = (mul_t(high_b, high_t) + (mul_t(high_b, low_t) + mul_t(low_b, high_t))) * (1.0 / width)
    row, lane = iota((count, LANES), 0), iota((count, LANES), 1)
    diagonal = jnp.sum(jnp.where(row == lane, gram, 0.0), axis=-1, keepdims=True)
    spread = jnp.where(row < pixels, gram, 2.0 * gram)
    spread = jnp.where(
        lane < pixels, spread, jnp.where((lane == pixels) & (row >= pixels), diagonal, 0.0)
    )
    folded = jnp.concatenate([spread, scores, values], axis=1)
    high_f, low_f = split(folded)
    rest = jnp.zeros((2 * LANES - 2 * count, folded.shape[1]), F32)
    return jnp.concatenate(
        [high_f[:pixels], low_f[:pixels], high_f[pixels:], low_f[pixels:], rest], axis=0
    ).astype(BF16)


def constants(fields, levels, width):
    variables = fields // levels
    pixels = variables * PATCH * PATCH
    heads = width // HEAD
    depth = variables * LANES
    source, target = iota((depth, LANES), 0), iota((depth, LANES), 1)
    place = (
        source // LANES * (PATCH * PATCH) + source % LANES // GROUP * PATCH + source % PATCH
    )
    column = source % GROUP // PATCH
    gather = jnp.concatenate(
        [jnp.where((target % pixels == place) & (column == b), 1.0, 0.0) for b in range(HALF)],
        axis=1,
    ).astype(BF16)
    count = HALF * levels * SLOT
    row, lane = iota((count, LANES), 0), iota((count, LANES), 1)
    level = jnp.where(
        (lane < 2 * levels) & (lane % levels == row // SLOT % levels), 1.0, 0.0
    ).astype(BF16)
    spread = jnp.concatenate(
        [
            jnp.where(
                iota((LANES, width), 0) == q * heads + iota((LANES, width), 1) // HEAD, 1.0, 0.0
            )
            for q in range(LATENT)
        ],
        axis=1,
    ).astype(BF16)
    return gather, level, spread


def aggregate_half(rows, folded, gather, level, spread):
    count = level.shape[0]
    levels = count // (HALF * SLOT)
    variables = rows.shape[0] // levels
    width = spread.shape[1] // LATENT
    pixels = variables * PATCH * PATCH
    order = member_order(rows.shape[0])
    wide = jnp.concatenate(
        [
            jnp.concatenate([rows[order.index(l * variables + v)] for l in range(levels)], axis=0)
            for v in range(variables)
        ],
        axis=1,
    ).astype(BF16)
    lane = iota((1, LANES), 1)
    parts = 2
    each = HALF // parts
    size = each * levels * SLOT
    patch = mul(wide, gather)
    stage = []
    for k in range(parts):
        part = jnp.concatenate(
            [patch[:, b * LANES : (b + 1) * LANES] for b in range(k * each, (k + 1) * each)], axis=0
        )
        full = jnp.concatenate([part.astype(BF16), level[:size]], axis=1)
        stage.append((part, full, mul(full, folded[:, : 2 * LANES])))
    ready = []
    for part, full, product in stage:
        moment, scores = product[:, :LANES], product[:, LANES:]
        values = mul(full, folded[:, 2 * LANES :])
        variance = jnp.sum(jnp.where(lane == pixels, 1.0, part) * moment, axis=-1, keepdims=True)
        scale = lax.rsqrt(jnp.maximum(variance, 0.0) + 1e-05)
        expo = jnp.exp2(scores * scale).reshape(each, levels, SLOT, LANES)
        weights = expo / jnp.sum(expo, axis=1, keepdims=True) * scale.reshape(each, levels, SLOT, 1)
        ready.append((weights.reshape(size, LANES).astype(BF16), values))
    pieces = [[] for _ in range(LATENT)]
    for weights, values in ready:
        for q in range(LATENT):
            part = mul(weights, spread[:, q * width : (q + 1) * width]) * values
            pieces[q].append(part.reshape(each, levels, SLOT, width).sum(axis=1).reshape(each * SLOT, width))
    mixed = [jnp.concatenate(p, axis=0) for p in pieces]
    return jnp.concatenate(mixed, axis=0)


def fold_window(query_ref, out_weight, qkv_weight):
    weight = out_weight.astype(F32)
    weight = weight - jnp.mean(weight, axis=-1, keepdims=True)
    through = mul(weight.astype(BF16), qkv_weight).astype(BF16)
    queries = query_ref[...].astype(F32)
    high, low = split(queries - jnp.mean(queries, axis=-1, keepdims=True))
    rest = jnp.zeros((16 - 2 * LATENT, queries.shape[1]), F32)
    base = mul(jnp.concatenate([high, low, rest], axis=0).astype(BF16), qkv_weight)
    base = base[:LATENT] + base[LATENT : 2 * LATENT]

    def by_token(value):
        latent = iota((HALF_ROWS, value.shape[1]), 0) // (WLAT * HALF)
        rows = jnp.zeros(latent.shape, F32)
        for q in range(LATENT):
            rows = jnp.where(latent == q, value[q : q + 1], rows)
        return rows

    return through, by_token(base), by_token(queries)


def tokens_of(attended, slots, clean, out_weight, through, base, queries):
    width = attended.shape[1]
    for c in range(width // LANES):
        slots[c, pl.ds(0, attended.shape[0]), :] = attended[:, c * LANES : (c + 1) * LANES]
    pairs = LATENT * WLAT
    for q in range(LATENT):
        for a in range(WLAT):
            for c in range(width // LANES):
                clean[pl.ds((q * WLAT + a) * HALF, HALF), pl.ds(c * LANES, LANES)] = slots[
                    c, pl.ds(q * HALF * SLOT + a, HALF, stride=SLOT), :
                ]
    clean[pl.ds(pairs * HALF, HALF_ROWS - pairs * HALF), :] = jnp.zeros(
        (HALF_ROWS - pairs * HALF, width), F32
    )
    tokens = clean[...].astype(BF16)
    shifted = (mul(tokens, out_weight) + queries).astype(BF16).astype(F32)
    qkv = mul(tokens, through) + base
    center = shifted - jnp.mean(shifted, axis=-1, keepdims=True)
    spread = jnp.mean(center * center, axis=-1, keepdims=True)
    return shifted, (qkv * lax.rsqrt(spread + 1e-05)).astype(BF16)


def own_kernel(
    block_ref, embed_ref, level_ref, query_ref, key_ref, value_ref, out_w_ref, qkv_w_ref,
    shifted_ref, qkv_ref, folded_ref, gather_ref, marks_ref, spread_ref, through_ref, base_ref,
    rows_ref, slots, clean,
):
    folded = fold_weights(embed_ref, level_ref, query_ref, key_ref, value_ref)
    folded_ref[...] = folded
    fields = block_ref.shape[0] // (2 * SLOT)
    gather, marks, spread = constants(fields, level_ref.shape[0], out_w_ref.shape[0])
    gather_ref[...] = gather
    marks_ref[...] = marks
    spread_ref[...] = spread
    through, base, queries = fold_window(query_ref, out_w_ref[...], qkv_w_ref[...])
    through_ref[...] = through
    base_ref[...] = base
    rows_ref[...] = queries
    rows = block_ref[...].astype(F32).reshape(fields, 2, SLOT, LANES)[:, 1]
    attended = aggregate_half(rows, folded, gather, marks, spread)
    shifted, qkv = tokens_of(attended, slots, clean, out_w_ref[...], through, base, queries)
    shifted_ref[...] = shifted
    qkv_ref[...] = qkv


def window_kernel(
    block_ref, shifted_ref, qkv_ref, folded_ref, gather_ref, marks_ref, spread_ref, through_ref,
    base_ref, rows_ref, out_w_ref, proj_w_ref, out_hbm, slots, clean, result, out_ref, sent,
):
    fields = block_ref.shape[0] // SLOT
    width = out_w_ref.shape[0]
    rows = block_ref[...].astype(F32).reshape(fields, SLOT, LANES)
    attended = aggregate_half(rows, folded_ref[...], gather_ref[...], marks_ref[...], spread_ref[...])
    shifted, qkv = tokens_of(
        attended, slots, clean, out_w_ref[...], through_ref[...], base_ref[...], rows_ref[...]
    )
    shifted = jnp.concatenate([shifted_ref[...], shifted], axis=0)
    qkv = jnp.concatenate([qkv_ref[...], qkv], axis=0)
    pairs = LATENT * WLAT
    row = iota((2 * HALF_ROWS, LANES), 0) % HALF_ROWS
    ones = jnp.where(row < pairs * HALF, 1.0, 0.0).astype(BF16)
    first = iota((1, LANES), 1) < HEAD
    mixed = []
    alls = []
    for p in range(width // LANES):
        queries = qkv[:, p * LANES : (p + 1) * LANES]
        keys = qkv[:, width + p * LANES : width + (p + 1) * LANES]
        values = qkv[:, 2 * width + p * LANES : 2 * width + (p + 1) * LANES]
        values = jnp.concatenate([values * BF16(2.0**-8), ones], axis=1)
        zero = jnp.zeros_like(queries)
        chosen = jnp.concatenate([jnp.where(first, queries, zero), jnp.where(first, zero, queries)], axis=0)
        scores = mul_t(chosen, keys)
        alls.append((jnp.exp2(scores * (HEAD ** (-0.5) * LOG2E)).astype(BF16), values))
    for expo, values in alls:
        found = mul(expo, values).reshape(2, 2 * HALF_ROWS, 2 * LANES)
        both = jnp.where(jnp.concatenate([first, first], axis=1), found[0], found[1])
        mixed.append((both[:, :LANES] / both[:, LANES:] * 2.0**8).astype(BF16))
    result[...] = shifted + mul(jnp.concatenate(mixed, axis=1), proj_w_ref[...])
    copies = [pltpu.make_async_copy(out_ref.at[q], out_hbm.at[q], sent.at[q]) for q in range(LATENT)]
    for i in range(pairs):
        out_ref[i // WLAT, i % WLAT] = jnp.concatenate(
            [result[pl.ds(i * HALF, HALF), :], result[pl.ds(HALF_ROWS + i * HALF, HALF), :]], axis=0
        ).astype(BF16)
        if i % WLAT == WLAT - 1:
            copies[i // WLAT].start()
    for copy in copies:
        copy.wait()


def whole(count):
    return [pl.BlockSpec(memory_space=pltpu.VMEM)] * count


def pack(pixels):
    _, count, _ = pixels.shape
    bands = count // (PATCH * WLAT)
    return pl.pallas_call(
        pack_kernel,
        out_shape=jax.ShapeDtypeStruct((bands * 2 * SLOT, LANES), BF16),
        in_specs=whole(1),
        out_specs=whole(1)[0],
        scratch_shapes=[pltpu.VMEM((2, count + 16, LANES), F32)],
        compiler_params=pltpu.CompilerParams(vmem_limit_bytes=8 * 2**20),
        cost_estimate=pl.CostEstimate(flops=8 * 10**9, bytes_accessed=2 * 10**5, transcendentals=0),
        name="pack",
    )(pixels[0].T)


def scratch(width):
    return [
        pltpu.VMEM((width // LANES, LATENT * HALF * SLOT + 3 * SLOT, LANES), F32),
        pltpu.VMEM((HALF_ROWS, width), F32),
    ]


def own_half(block, embed_weight, level_code, queries, w_key, w_value, w_out, w_qkv):
    width = w_out.shape[0]
    fields, levels = block.shape[0], level_code.shape[0]
    return pl.pallas_call(
        own_kernel,
        out_shape=[
            jax.ShapeDtypeStruct((HALF_ROWS, width), F32),
            jax.ShapeDtypeStruct((HALF_ROWS, w_qkv.shape[1]), BF16),
            jax.ShapeDtypeStruct((2 * LANES, width + 2 * LANES), BF16),
            jax.ShapeDtypeStruct((fields // levels * LANES, HALF * LANES), BF16),
            jax.ShapeDtypeStruct((HALF * levels * SLOT, LANES), BF16),
            jax.ShapeDtypeStruct((LANES, LATENT * width), BF16),
            jax.ShapeDtypeStruct(w_qkv.shape, BF16),
            jax.ShapeDtypeStruct((HALF_ROWS, w_qkv.shape[1]), F32),
            jax.ShapeDtypeStruct((HALF_ROWS, width), F32),
        ],
        in_specs=whole(8),
        out_specs=whole(9),
        scratch_shapes=scratch(width),
        compiler_params=pltpu.CompilerParams(vmem_limit_bytes=24 * 2**20),
        cost_estimate=pl.CostEstimate(flops=4 * 10**9, bytes_accessed=2 * 10**6, transcendentals=0),
        name="own_half",
    )(
        block.reshape(-1, LANES), embed_weight.reshape(-1, width), level_code, queries, w_key, w_value,
        w_out, w_qkv,
    )


def window(east, own, w_out, w_proj):
    width = w_out.shape[0]
    return pl.pallas_call(
        window_kernel,
        out_shape=jax.ShapeDtypeStruct((LATENT, WLAT, WLON, width), BF16),
        in_specs=whole(12),
        out_specs=pl.BlockSpec(memory_space=pltpu.HBM),
        scratch_shapes=scratch(width)
        + [
            pltpu.VMEM((2 * HALF_ROWS, width), F32),
            pltpu.VMEM((LATENT, WLAT, WLON, width), BF16),
            pltpu.SemaphoreType.DMA((LATENT,)),
        ],
        compiler_params=pltpu.CompilerParams(vmem_limit_bytes=32 * 2**20),
        cost_estimate=pl.CostEstimate(flops=8 * 10**9, bytes_accessed=4 * 10**6, transcendentals=0),
        name="window",
    )(east.reshape(-1, LANES), *own, w_out, w_proj)


def western_pairs(bands, sectors):
    pairs = []
    for g in range(bands):
        for l in range(sectors):
            source = (g + l % 2 * (bands // 2)) % bands
            pairs.append((source * sectors + (l + 1) % sectors, g * sectors + l))
    return pairs


def body(pixels, embed_weight, level_code, queries, w_key, w_value, w_out, w_qkv, w_proj):
    packed = pack(pixels)
    bands, sectors = lax.axis_size("var"), lax.axis_size("lon")
    block = lax.all_to_all(
        packed.reshape(bands, 2 * SLOT, LANES),
        "var",
        split_axis=0,
        concat_axis=0,
        axis_index_groups=[member_order(bands)],
        tiled=True,
    )
    east = lax.ppermute(block[:, :SLOT], ("var", "lon"), western_pairs(bands, sectors))
    own = own_half(block, embed_weight, level_code, queries, w_key, w_value, w_out, w_qkv)
    return window(east, own, w_out, w_proj)


def solution(mesh):
    placed = (P("var", None, "lon"), P(), P(), P(), P(), P(), P(), P(), P())
    return jax.shard_map(
        body, mesh=mesh, in_specs=placed, out_specs=P(None, "var", "lon", None), check_vma=False
    )
```
